32 devices in a mesh: dp: 16 (over z, x, core), expert: 2 (over y).
Axes of the slice: x: 2, y: 2, z: 4, core: 2. Of those that a mesh axis runs over, the one named last changes fastest.
Arguments:
- tokens: bfloat16 [2048, 2048], P('dp'), may hold values from -6 to 6
- routes: int32 [2048, 8], P('dp'), may hold values from 0 to 15, all different within a row; in each aligned block of 128 rows (0 to 127, 128 to 255, ...) at most 64 rows name the same one
- kept_mask: int32 [2048, 8], P('dp'), may hold values from 0 to 1, as said below
- gate_probs: float32 [2048, 8], P('dp'), may hold values from 0.05 to 0.5
- output_grad: bfloat16 [2048, 2048], P('dp'), may hold values from -96 to 96
- w_gate: bfloat16 [16, 2048, 1024], P('dp', None, 'expert'), may hold values from -0.125 to 0.125
- w_up: bfloat16 [16, 2048, 1024], P('dp', None, 'expert'), may hold values from -0.125 to 0.125
- w_down: bfloat16 [16, 1024, 2048], P('dp', 'expert'), may hold values from -0.1875 to 0.1875
Outputs:
- output: bfloat16 [2048, 2048], P('dp', 'expert')
- input_grad: bfloat16 [2048, 2048], P('dp', 'expert')
- grad_gate: bfloat16 [16, 2048, 1024], P('dp', None, 'expert')
- grad_up: bfloat16 [16, 2048, 1024], P('dp', None, 'expert')
- grad_down: bfloat16 [16, 1024, 2048], P('dp', 'expert')
The draws below stay inside these ranges and needn't reach their ends.
Inputs may be any that keep to these rules, and one draw needn't show every extreme that they name: `routes`: each row names 8 different experts, and the 128 rows of each index of dp name every expert exactly 64 times. `kept_mask`: the share of kept entries varies along the tokens.
All inputs are finite; a program needn't handle non-finite values.
Results may differ from the reference program's by a relative error of at most 0.0064.
Values may be sent and summed in bfloat16 or wider, within the bound.
No kernel may reach another device: no remote copies, remote signals or barrier semaphores. Data moves between devices by JAX's collectives and lax.ppermute only.
A program may use at most 128 MiB of HBM per device.

```python
import math
import jax
import jax.numpy as jnp
import numpy as np
from jax import lax

D = 2048
HIDDEN_SIZE = 1024
TOPK = 8
TOK = 128
EXPERTS = 16
TOKENS = 2048
CAP = 64
SLOTS = 1024
N_DP = 16


def draw_kept_mask(key, part):
    row_ids = jnp.arange(TOKENS, dtype=jnp.int32)[:, None]
    level = 300 + 650 * row_ids // TOKENS
    ticket = jax.random.randint(key, (TOKENS, TOPK), 0, 1000, dtype=jnp.int32)
    return (ticket < level).astype(jnp.int32)


def steps_of(stream_key, shape, pieces, smallest, top_value):
    loudness, own = 1.0, jax.random.fold_in(stream_key, 6)
    for axis_at, shards_of in pieces:
        heights = jnp.exp(jax.random.uniform(jax.random.fold_in(own, axis_at), (shards_of,), jnp.float32, smallest / len(pieces), top_value / len(pieces)))
        loudness = loudness * jnp.repeat(heights, shape[axis_at] // shards_of).reshape([-1 if axis == axis_at else 1 for axis in range(len(shape))])
    return loudness


def assign_block(key, own, number, rows, number_of, top, most, slope):
    sequence = jax.random.permutation(key, number_of)
    heavy_load, ordinary = load_shares(number_of, rows * top, most, slope, True), load_shares(number_of, rows * top, most, slope, False)
    places = jnp.arange(number_of)

    def named(tallies, rotation):
        used = int((tallies > 0).sum())
        fixed = max(1, used // 4)
        shifted = fixed + (places - fixed + rotation * (used - fixed)) % max(1, number_of - fixed)
        return jnp.zeros((number_of,), jnp.int32).at[sequence[jnp.where(places < fixed, places, shifted)]].set(jnp.asarray(tallies, jnp.int32))

    tallies = jnp.where(number % 4 == 0, named(heavy_load, number // 4), named(ordinary, number - number // 4 - 1))
    mixed = jax.random.permutation(jax.random.fold_in(own, 3), number_of)
    donor, taker = mixed[0:number_of // 2 * 2:2], mixed[1:number_of // 2 * 2:2]
    slack = jnp.minimum(tallies[donor] - 1, most - tallies[taker]) // 2
    slack = jnp.where((donor == sequence[0]) | (taker == sequence[0]) | (tallies[taker] == 0), 0, jnp.maximum(slack, 0))
    shifted = jax.random.randint(jax.random.fold_in(own, 4), (number_of // 2,), 0, 1 << 20) % (slack + 1)
    tallies = tallies.at[donor].add(-shifted).at[taker].add(shifted)
    items = jnp.searchsorted(jnp.cumsum(tallies), jnp.arange(rows * top), side="right").astype(jnp.int32)
    table = items.reshape(top, rows).T
    table = table[jax.random.permutation(jax.random.fold_in(own, 1), rows)]
    rotation = jax.random.randint(jax.random.fold_in(own, 2), (rows, 1), 0, top)
    return jnp.take_along_axis(table, (jnp.arange(top)[None, :] + rotation) % top, axis=1)


def load_shares(count, total, most, slope, full):
    loads = [(1 << 20) // math.isqrt(rank ** slope) + 1 for rank in range(1, count + 1)]
    largest = most if full else min(most, max(-(-total // count), total * loads[0] // sum(loads)))
    least = 1 if total - largest >= count - 1 else 0
    given, spare = [largest] + [least] * (count - 1), total - largest - least * (count - 1)
    while spare > 0:
        candidates = [i for i in range(1, count) if given[i] < largest] or [i for i in range(1, count) if given[i] < most]
        whole, budget = sum([loads[i] for i in candidates]), spare
        for i in candidates:
            more = min(most - given[i], max(1, budget * loads[i] // whole), spare)
            given[i] = given[i] + more
            spare = spare - more
    return np.array(given)


def scatter_about(rng, shape, spread, bound, pieces=(), kind=jnp.bfloat16):
    factor_of = steps_of(rng, shape, pieces, -0.22, 0.18) if pieces else 1.0
    result = jax.random.normal(rng, shape, jnp.float32) * spread * factor_of
    return jnp.minimum(jnp.maximum(result, -bound), bound).astype(kind)


def setup_inputs(seed: int = 0) -> dict:
    seeds = jax.random.split(jax.random.key(seed), 9)
    tokens = scatter_about(seeds[0], (TOKENS, D), 1.0, 6.0, ((0, 16),))
    routes_keys = jax.random.split(jax.random.fold_in(seeds[1], 1), TOKENS // TOK)
    routes_turns = jax.random.permutation(jax.random.fold_in(seeds[1], 3), TOKENS // TOK)
    routes = jax.vmap(lambda own, number: assign_block(jax.random.fold_in(seeds[1], 2), own, number, TOK, EXPERTS, TOPK, CAP, 0))(routes_keys, routes_turns).reshape((TOKENS, TOPK))
    kept_mask = draw_kept_mask(jax.random.fold_in(seeds[8], 71), 0)
    gate_probs = jnp.clip(0.05 + 0.45 * jax.random.uniform(seeds[3], (TOKENS, TOPK), jnp.float32) ** steps_of(seeds[3], (TOKENS, TOPK), ((0, 16),), -0.2, 0.2), 0.05, 0.5)
    output_grad = scatter_about(seeds[4], (TOKENS, D), 16.0, 96.0, ((0, 16),))
    w_gate = scatter_about(seeds[5], (EXPERTS, D, HIDDEN_SIZE), D ** -0.5, 0.125, ((0, 16), (2, 2)))
    w_up = scatter_about(seeds[6], (EXPERTS, D, HIDDEN_SIZE), D ** -0.5, 0.125, ((0, 16), (2, 2)))
    w_down = scatter_about(seeds[7], (EXPERTS, HIDDEN_SIZE, D), HIDDEN_SIZE ** -0.5, 0.1875, ((0, 16), (1, 2)))
    return {"tokens": tokens, "routes": routes, "kept_mask": kept_mask, "gate_probs": gate_probs, "output_grad": output_grad, "w_gate": w_gate, "w_up": w_up, "w_down": w_down}


def silu_parts(gate_val):
    sigmoid_val = jax.nn.sigmoid(gate_val)
    return gate_val * sigmoid_val, sigmoid_val * (1.0 + gate_val * (1.0 - sigmoid_val))


def reference(tokens, routes, kept_mask, gate_probs, output_grad, w_gate, w_up, w_down):
    pair_count = TOKENS * TOPK
    flat_routes = routes.reshape(N_DP, TOK * TOPK)
    onehot = (flat_routes[:, :, None] == jnp.arange(EXPERTS, dtype=jnp.int32)[None, None, :]).astype(jnp.int32)
    before = jnp.cumsum(onehot, axis=1) - onehot
    slot_index = jnp.sum(before * onehot, axis=2)
    shard_base = (jnp.arange(N_DP, dtype=jnp.int32) * CAP)[:, None]
    dest_index = (flat_routes * SLOTS + shard_base + slot_index).reshape(pair_count).astype(jnp.int32)
    source = jnp.zeros((pair_count,), jnp.int32).at[dest_index].set(jnp.arange(pair_count, dtype=jnp.int32))
    keep_float = kept_mask.reshape(pair_count).astype(jnp.float32)
    weight_flat = keep_float * gate_probs.reshape(pair_count)
    kept_count = jnp.sum(onehot.astype(jnp.float32) * keep_float.reshape(N_DP, TOK * TOPK, 1), axis=(0, 1))
    src_token = (source // TOPK).reshape(EXPERTS, SLOTS)
    src_keep = keep_float[source].reshape(EXPERTS, SLOTS)
    src_weight = weight_flat[source].reshape(EXPERTS, SLOTS)

    def one_expert(bundle):
        gate_w, up_w, down_w, token_ids, keep_rows, weight_rows, expert_count = bundle
        expert_in = (tokens[token_ids].astype(jnp.float32) * keep_rows[:, None]).astype(jnp.bfloat16)
        cot_rows = (output_grad[token_ids].astype(jnp.float32) * weight_rows[:, None]).astype(jnp.bfloat16)
        gate_val = jnp.dot(expert_in, gate_w, preferred_element_type=jnp.float32)
        up_val = jnp.dot(expert_in, up_w, preferred_element_type=jnp.float32)
        act_val, act_slope = silu_parts(gate_val)
        hidden = (act_val * up_val).astype(jnp.bfloat16)
        expert_out = jnp.dot(hidden, down_w, preferred_element_type=jnp.float32).astype(jnp.bfloat16)
        d_hidden = jnp.dot(cot_rows, down_w.T, preferred_element_type=jnp.float32)
        d_gate = (d_hidden * up_val * act_slope).astype(jnp.bfloat16)
        d_up = (d_hidden * act_val).astype(jnp.bfloat16)
        inv_count = 1.0 / jnp.maximum(expert_count, 1.0)
        grad_down = (jnp.dot(hidden.T, cot_rows, preferred_element_type=jnp.float32) * inv_count).astype(jnp.bfloat16)
        grad_gate = (jnp.dot(expert_in.T, d_gate, preferred_element_type=jnp.float32) * inv_count).astype(jnp.bfloat16)
        grad_up = (jnp.dot(expert_in.T, d_up, preferred_element_type=jnp.float32) * inv_count).astype(jnp.bfloat16)
        d_rows = (jnp.dot(d_gate, gate_w.T, preferred_element_type=jnp.float32)
                  + jnp.dot(d_up, up_w.T, preferred_element_type=jnp.float32)).astype(jnp.bfloat16)
        return expert_out, d_rows, grad_gate, grad_up, grad_down

    expert_out, d_rows, grad_gate, grad_up, grad_down = lax.map(
        one_expert, (w_gate, w_up, w_down, src_token, src_keep, src_weight, kept_count))
    out_rows = expert_out.reshape(pair_count, D)[dest_index].astype(jnp.float32) * weight_flat[:, None]
    output = jnp.sum(out_rows.reshape(TOKENS, TOPK, D), axis=1).astype(jnp.bfloat16)
    grad_rows = d_rows.reshape(pair_count, D)[dest_index].astype(jnp.float32) * keep_float[:, None]
    input_grad = jnp.sum(grad_rows.reshape(TOKENS, TOPK, D), axis=1).astype(jnp.bfloat16)
    return output, input_grad, grad_gate, grad_up, grad_down
```

```python
import jax
import jax.numpy as jnp
from jax import lax
from jax.sharding import PartitionSpec as P


def silu_parts(gate_val):
    sigmoid_val = jax.nn.sigmoid(gate_val)
    return (gate_val * sigmoid_val, sigmoid_val * (1.0 + gate_val * (1.0 - sigmoid_val)))


def slot_layout(routes, experts):
    tok_rows, top_count = routes.shape
    pair_count = tok_rows * top_count
    flat_routes = routes.reshape(pair_count)
    onehot = (flat_routes[:, None] == jnp.arange(experts, dtype=jnp.int32)[None, :]).astype(
        jnp.int32
    )
    before = jnp.cumsum(onehot, axis=0) - onehot
    slot_index = jnp.sum(before * onehot, axis=1)
    capacity = pair_count // experts
    dest_index = flat_routes * capacity + slot_index
    source = (
        jnp.zeros((pair_count,), jnp.int32)
        .at[dest_index]
        .set(jnp.arange(pair_count, dtype=jnp.int32))
    )
    return (dest_index, source, onehot)


def to_experts(rows_in, dp_size, local_experts):
    capacity = rows_in.shape[1]
    width = rows_in.shape[2]
    grouped = rows_in.reshape(dp_size, local_experts, capacity, width)
    return jnp.swapaxes(grouped, 0, 1).reshape(local_experts, dp_size * capacity, width)


def from_experts(values, dp_size):
    local_experts, slot_total, width = values.shape
    capacity = slot_total // dp_size
    grouped = values.reshape(local_experts, dp_size, capacity, width)
    return jnp.swapaxes(grouped, 0, 1).reshape(dp_size * local_experts, capacity, width)


def combine(back_rows, dest_index, factor, tok_rows, top_count):
    width = back_rows.shape[2]
    picked = back_rows.reshape(-1, width)[dest_index].astype(jnp.float32) * factor[:, None]
    return jnp.sum(picked.reshape(tok_rows, top_count, width), axis=1)


def routed_plan(tokens, routes, kept_mask, gate_probs, output_grad, w_gate, w_up, w_down):
    dp_size = lax.axis_size("dp")
    part_count = lax.axis_size("expert")
    local_experts, model_width, hidden_part = w_gate.shape
    experts = local_experts * dp_size
    tok_rows, top_count = routes.shape
    capacity = tok_rows * top_count // experts
    col_width = model_width // part_count
    dest_index, source, onehot = slot_layout(routes, experts)
    keep_float = kept_mask.reshape(-1).astype(jnp.float32)
    weight_flat = keep_float * gate_probs.reshape(-1)
    src_token = source // top_count
    src_keep = keep_float[source]
    src_weight = weight_flat[source]
    col_start = lax.axis_index("expert") * col_width
    token_src = lax.dynamic_slice_in_dim(tokens, col_start, col_width, 1)
    cot_src = lax.dynamic_slice_in_dim(output_grad, col_start, col_width, 1)
    send_width = token_src.shape[1]
    rows_send = (token_src[src_token].astype(jnp.float32) * src_keep[:, None]).astype(jnp.bfloat16)
    rows_send = rows_send.reshape(experts, capacity, send_width)
    cot_send = (cot_src[src_token].astype(jnp.float32) * src_weight[:, None]).astype(jnp.bfloat16)
    cot_send = cot_send.reshape(experts, capacity, send_width)
    totals = jnp.sum(onehot.astype(jnp.float32) * keep_float[:, None], axis=0)
    totals = lax.psum(totals, "dp")
    kept_count = lax.dynamic_slice_in_dim(
        totals, lax.axis_index("dp") * local_experts, local_experts
    )
    rows_in = lax.all_to_all(rows_send, "dp", split_axis=0, concat_axis=0, tiled=True)
    cot_in = lax.all_to_all(cot_send, "dp", split_axis=0, concat_axis=0, tiled=True)
    rows_in = lax.all_gather(rows_in, "expert", axis=2, tiled=True)
    cot_in = lax.all_gather(cot_in, "expert", axis=2, tiled=True)
    expert_in = to_experts(rows_in, dp_size, local_experts)
    cot_full = to_experts(cot_in, dp_size, local_experts)
    down_cols = lax.all_to_all(w_down, "expert", split_axis=2, concat_axis=1, tiled=True)
    gate_rows, up_rows = (
        lax.all_to_all(w_gate, "expert", split_axis=1, concat_axis=2, tiled=True),
        lax.all_to_all(w_up, "expert", split_axis=1, concat_axis=2, tiled=True),
    )
    gate_val = jnp.einsum("lsd,ldh->lsh", expert_in, w_gate, preferred_element_type=jnp.float32)
    up_val = jnp.einsum("lsd,ldh->lsh", expert_in, w_up, preferred_element_type=jnp.float32)
    act_val, act_slope = silu_parts(gate_val)
    hidden = (act_val * up_val).astype(jnp.bfloat16)
    expert_out = jnp.einsum(
        "lsh,lhc->lsc",
        lax.all_gather(hidden, "expert", axis=2, tiled=True),
        down_cols,
        preferred_element_type=jnp.float32,
    ).astype(jnp.bfloat16)
    out_back = lax.all_to_all(
        from_experts(expert_out, dp_size), "dp", split_axis=0, concat_axis=0, tiled=True
    )
    output = combine(out_back, dest_index, weight_flat, tok_rows, top_count).astype(jnp.bfloat16)
    d_hidden = jnp.einsum("lsd,lhd->lsh", cot_full, w_down, preferred_element_type=jnp.float32)
    d_gate = (d_hidden * up_val * act_slope).astype(jnp.bfloat16)
    d_up = (d_hidden * act_val).astype(jnp.bfloat16)
    inv_count = (1.0 / jnp.maximum(kept_count, 1.0))[:, None, None]
    grad_down = (
        jnp.einsum("lsh,lsd->lhd", hidden, cot_full, preferred_element_type=jnp.float32) * inv_count
    ).astype(jnp.bfloat16)
    grad_gate = (
        jnp.einsum("lsd,lsh->ldh", expert_in, d_gate, preferred_element_type=jnp.float32)
        * inv_count
    ).astype(jnp.bfloat16)
    grad_up = (
        jnp.einsum("lsd,lsh->ldh", expert_in, d_up, preferred_element_type=jnp.float32) * inv_count
    ).astype(jnp.bfloat16)
    running = jnp.einsum(
        "lsh,lch->lsc",
        lax.all_gather(d_gate, "expert", axis=2, tiled=True),
        gate_rows,
        preferred_element_type=jnp.float32,
    )
    d_rows = (
        running
        + jnp.einsum(
            "lsh,lch->lsc",
            lax.all_gather(d_up, "expert", axis=2, tiled=True),
            up_rows,
            preferred_element_type=jnp.float32,
        )
    ).astype(jnp.bfloat16)
    grad_back = lax.all_to_all(
        from_experts(d_rows, dp_size), "dp", split_axis=0, concat_axis=0, tiled=True
    )
    input_grad = combine(grad_back, dest_index, keep_float, tok_rows, top_count).astype(
        jnp.bfloat16
    )
    return (output, input_grad, grad_gate, grad_up, grad_down)


def swap(values, axis_name, bit):
    size = lax.axis_size(axis_name)
    return lax.ppermute(values, axis_name, [(i, i ^ bit) for i in range(size)])


def shift(values, steps):
    size = lax.axis_size("dp")
    return lax.ppermute(values, "dp", [(i, (i + 4 * steps) % size) for i in range(size)])


def own_half(values):
    rows = values.shape[0] // 2
    return lax.dynamic_slice_in_dim(values, lax.axis_index("expert") * rows, rows, 0)


def gather_line(block, line):
    pieces = []
    current = block
    for step in range(line):
        following = shift(current, 1) if step < line - 1 else None
        from_x = swap(own_half(current), "dp", 2)
        from_y = swap(from_x, "expert", 1)
        mine = jnp.concatenate([current, from_x, from_y], axis=0)
        pieces.append((mine, swap(mine, "dp", 1)))
        current = following
    return pieces


def gather_small(values, line):
    pair = jnp.stack([values, swap(values, "dp", 1)])
    quad = jnp.stack([pair, swap(pair, "dp", 2)])
    return jnp.stack([quad] + [shift(quad, step) for step in range(1, line)])


def add_bf16(a, b):
    return (a.astype(jnp.float32) + b.astype(jnp.float32)).astype(jnp.bfloat16)


def send_home(contrib, step):
    summed = add_bf16(contrib[:, :, 0], swap(contrib[:, :, 1], "dp", 1))
    if step % 2 == 0:
        summed = add_bf16(summed[:, 0], swap(summed[:, 1], "dp", 2))
        summed = add_bf16(summed[0], swap(summed[1], "expert", 1))
    else:
        summed = add_bf16(summed[0], swap(summed[1], "expert", 1))
        summed = add_bf16(summed[0], swap(summed[1], "dp", 2))
    return shift(summed, -step) if step else summed


def dense_plan(tokens, routes, kept_mask, gate_probs, output_grad, w_gate, w_up, w_down):
    dp_size = lax.axis_size("dp")
    line = dp_size // 4
    tok_rows, top_count = routes.shape
    capacity = tok_rows * top_count // dp_size
    model_width = tokens.shape[1]
    part = lax.axis_index("expert")
    w_gate, w_up, w_down = w_gate[0], w_up[0], w_down[0]

    table = jnp.concatenate(
        [routes.T.astype(jnp.float32), kept_mask.T.astype(jnp.float32), gate_probs.T], axis=0
    )
    table = gather_small(table, line)
    chosen, kept, probs = jnp.split(table, 3, axis=3)
    expert = lax.axis_index("dp").astype(jnp.float32)
    hit = jnp.where(chosen == expert, kept, 0.0)
    used = jnp.sum(hit, axis=3)
    weight = jnp.sum(hit * probs, axis=3)
    kept_count = jnp.sum(used)
    earlier = jnp.triu(jnp.ones((tok_rows, tok_rows), jnp.bfloat16), 1)
    rank = jnp.einsum(
        "sabt,tu->sabu", used.astype(jnp.bfloat16), earlier, preferred_element_type=jnp.float32
    )
    slots = jnp.arange(capacity, dtype=jnp.float32)[:, None]
    pick = jnp.where(rank[..., None, :] == slots, used[..., None, :], 0.0)
    row_weight = jnp.sum(pick * weight[..., None, :], axis=4)
    pick = pick.astype(jnp.bfloat16)
    turned = jnp.where(part == 0, pick[:, 1], jnp.roll(pick[:, 1], tok_rows // 2, axis=3))
    pick_in = jnp.stack([pick[:, 0], turned], axis=1)

    token_pieces = gather_line(tokens, line)
    cot_pieces = gather_line(output_grad, line)

    def rows_of(piece, step):
        both = jnp.stack(piece).reshape(2, 2, tok_rows, model_width)
        return jnp.einsum(
            "abrt,batd->abrd", pick_in[step], both, preferred_element_type=jnp.float32
        )

    def spread(rows, step):
        out = jnp.einsum(
            "abrt,abrd->abtd",
            pick[step],
            rows.reshape(2, 2, capacity, model_width),
            preferred_element_type=jnp.float32,
        ).astype(jnp.bfloat16)
        out = out.reshape(2, 2, tok_rows, 2, model_width // 2)
        mine = lax.dynamic_index_in_dim(out, part, 3, keepdims=False)
        theirs = lax.dynamic_index_in_dim(out, 1 - part, 3, keepdims=False)
        return jnp.stack([mine, theirs])

    def dot(a, b, dims):
        return lax.dot_general(a, b, (dims, ((), ())), preferred_element_type=jnp.float32)

    saved, outputs, grads = [], [], []
    for step in range(line):
        expert_in = rows_of(token_pieces[step], step).astype(jnp.bfloat16).reshape(-1, model_width)
        gate_val = dot(expert_in, w_gate, ((1,), (0,)))
        up_val = dot(expert_in, w_up, ((1,), (0,)))
        act_val, act_slope = silu_parts(gate_val)
        hidden = (act_val * up_val).astype(jnp.bfloat16)
        scale = row_weight[step].reshape(-1, 1)
        expert_out = (dot(hidden, w_down, ((1,), (0,))) * scale).astype(jnp.bfloat16)
        outputs.append(send_home(spread(expert_out, step), step))
        saved.append((expert_in, up_val, act_val, act_slope, hidden))
    finals = []
    for step in range(line):
        expert_in, up_val, act_val, act_slope, hidden = saved[step]
        scale = row_weight[step][..., None]
        cot_rows = (rows_of(cot_pieces[step], step) * scale).astype(jnp.bfloat16)
        cot_rows = cot_rows.reshape(-1, model_width)
        d_hidden = dot(cot_rows, w_down, ((1,), (1,)))
        d_gate = (d_hidden * up_val * act_slope).astype(jnp.bfloat16)
        d_up = (d_hidden * act_val).astype(jnp.bfloat16)
        d_rows = dot(d_gate, w_gate, ((1,), (1,))) + dot(d_up, w_up, ((1,), (1,)))
        grads.append(send_home(spread(d_rows.astype(jnp.bfloat16), step), step))
        finals.append((expert_in, hidden, cot_rows, d_gate, d_up))
    expert_in, hidden, cot_rows, d_gate, d_up = (
        jnp.concatenate(parts, axis=0) for parts in zip(*finals)
    )
    inv_count = 1.0 / jnp.maximum(kept_count, 1.0)
    grad_down = (dot(hidden, cot_rows, ((0,), (0,))) * inv_count).astype(jnp.bfloat16)
    grad_gate = (dot(expert_in, d_gate, ((0,), (0,))) * inv_count).astype(jnp.bfloat16)
    grad_up = (dot(expert_in, d_up, ((0,), (0,))) * inv_count).astype(jnp.bfloat16)
    output = sum(part_sum.astype(jnp.float32) for part_sum in outputs).astype(jnp.bfloat16)
    input_grad = sum(part_sum.astype(jnp.float32) for part_sum in grads).astype(jnp.bfloat16)
    return (output, input_grad, grad_gate[None], grad_up[None], grad_down[None])


def per_device(tokens, routes, kept_mask, gate_probs, output_grad, w_gate, w_up, w_down):
    dp_size = lax.axis_size("dp")
    local_experts = w_gate.shape[0]
    top_count = routes.shape[1]
    dense = (
        local_experts == 1
        and lax.axis_size("expert") == 2
        and dp_size % 4 == 0
        and 2 * top_count >= dp_size
    )
    plan = dense_plan if dense else routed_plan
    return plan(tokens, routes, kept_mask, gate_probs, output_grad, w_gate, w_up, w_down)


def solution(mesh):
    placed = (
        P("dp", None),
        P("dp", None),
        P("dp", None),
        P("dp", None),
        P("dp", None),
        P("dp", None, "expert"),
        P("dp", None, "expert"),
        P("dp", "expert", None),
    )
    return jax.shard_map(
        per_device,
        mesh=mesh,
        in_specs=placed,
        out_specs=(
            P("dp", "expert"),
            P("dp", "expert"),
            P("dp", None, "expert"),
            P("dp", None, "expert"),
            P("dp", "expert", None),
        ),
        check_vma=False,
    )
```

```python
import functools
import math

import jax
import jax.numpy as jnp
from jax import lax
from jax.experimental import pallas as pl
from jax.experimental.pallas import tpu as pltpu
from jax.sharding import PartitionSpec as P


def silu_parts(gate_val):
    sigmoid_val = jax.nn.sigmoid(gate_val)
    return (gate_val * sigmoid_val, sigmoid_val * (1.0 + gate_val * (1.0 - sigmoid_val)))


def slot_layout(routes, experts):
    tok_rows, top_count = routes.shape
    pair_count = tok_rows * top_count
    flat_routes = routes.reshape(pair_count)
    onehot = (flat_routes[:, None] == jnp.arange(experts, dtype=jnp.int32)[None, :]).astype(
        jnp.int32
    )
    before = jnp.cumsum(onehot, axis=0) - onehot
    slot_index = jnp.sum(before * onehot, axis=1)
    capacity = pair_count // experts
    dest_index = flat_routes * capacity + slot_index
    source = (
        jnp.zeros((pair_count,), jnp.int32)
        .at[dest_index]
        .set(jnp.arange(pair_count, dtype=jnp.int32))
    )
    return (dest_index, source, onehot)


def to_experts(rows_in, dp_size, local_experts):
    capacity = rows_in.shape[1]
    width = rows_in.shape[2]
    grouped = rows_in.reshape(dp_size, local_experts, capacity, width)
    return jnp.swapaxes(grouped, 0, 1).reshape(local_experts, dp_size * capacity, width)


def from_experts(values, dp_size):
    local_experts, slot_total, width = values.shape
    capacity = slot_total // dp_size
    grouped = values.reshape(local_experts, dp_size, capacity, width)
    return jnp.swapaxes(grouped, 0, 1).reshape(dp_size * local_experts, capacity, width)


def combine(back_rows, dest_index, factor, tok_rows, top_count):
    width = back_rows.shape[2]
    picked = back_rows.reshape(-1, width)[dest_index].astype(jnp.float32) * factor[:, None]
    return jnp.sum(picked.reshape(tok_rows, top_count, width), axis=1)


def routed_plan(tokens, routes, kept_mask, gate_probs, output_grad, w_gate, w_up, w_down):
    dp_size = lax.axis_size("dp")
    part_count = lax.axis_size("expert")
    local_experts, model_width, hidden_part = w_gate.shape
    experts = local_experts * dp_size
    tok_rows, top_count = routes.shape
    capacity = tok_rows * top_count // experts
    col_width = model_width // part_count
    dest_index, source, onehot = slot_layout(routes, experts)
    keep_float = kept_mask.reshape(-1).astype(jnp.float32)
    weight_flat = keep_float * gate_probs.reshape(-1)
    src_token = source // top_count
    src_keep = keep_float[source]
    src_weight = weight_flat[source]
    col_start = lax.axis_index("expert") * col_width
    token_src = lax.dynamic_slice_in_dim(tokens, col_start, col_width, 1)
    cot_src = lax.dynamic_slice_in_dim(output_grad, col_start, col_width, 1)
    send_width = token_src.shape[1]
    rows_send = (token_src[src_token].astype(jnp.float32) * src_keep[:, None]).astype(jnp.bfloat16)
    rows_send = rows_send.reshape(experts, capacity, send_width)
    cot_send = (cot_src[src_token].astype(jnp.float32) * src_weight[:, None]).astype(jnp.bfloat16)
    cot_send = cot_send.reshape(experts, capacity, send_width)
    totals = jnp.sum(onehot.astype(jnp.float32) * keep_float[:, None], axis=0)
    totals = lax.psum(totals, "dp")
    kept_count = lax.dynamic_slice_in_dim(
        totals, lax.axis_index("dp") * local_experts, local_experts
    )
    rows_in = lax.all_to_all(rows_send, "dp", split_axis=0, concat_axis=0, tiled=True)
    cot_in = lax.all_to_all(cot_send, "dp", split_axis=0, concat_axis=0, tiled=True)
    rows_in = lax.all_gather(rows_in, "expert", axis=2, tiled=True)
    cot_in = lax.all_gather(cot_in, "expert", axis=2, tiled=True)
    expert_in = to_experts(rows_in, dp_size, local_experts)
    cot_full = to_experts(cot_in, dp_size, local_experts)
    down_cols = lax.all_to_all(w_down, "expert", split_axis=2, concat_axis=1, tiled=True)
    gate_rows, up_rows = (
        lax.all_to_all(w_gate, "expert", split_axis=1, concat_axis=2, tiled=True),
        lax.all_to_all(w_up, "expert", split_axis=1, concat_axis=2, tiled=True),
    )
    gate_val = jnp.einsum("lsd,ldh->lsh", expert_in, w_gate, preferred_element_type=jnp.float32)
    up_val = jnp.einsum("lsd,ldh->lsh", expert_in, w_up, preferred_element_type=jnp.float32)
    act_val, act_slope = silu_parts(gate_val)
    hidden = (act_val * up_val).astype(jnp.bfloat16)
    expert_out = jnp.einsum(
        "lsh,lhc->lsc",
        lax.all_gather(hidden, "expert", axis=2, tiled=True),
        down_cols,
        preferred_element_type=jnp.float32,
    ).astype(jnp.bfloat16)
    out_back = lax.all_to_all(
        from_experts(expert_out, dp_size), "dp", split_axis=0, concat_axis=0, tiled=True
    )
    output = combine(out_back, dest_index, weight_flat, tok_rows, top_count).astype(jnp.bfloat16)
    d_hidden = jnp.einsum("lsd,lhd->lsh", cot_full, w_down, preferred_element_type=jnp.float32)
    d_gate = (d_hidden * up_val * act_slope).astype(jnp.bfloat16)
    d_up = (d_hidden * act_val).astype(jnp.bfloat16)
    inv_count = (1.0 / jnp.maximum(kept_count, 1.0))[:, None, None]
    grad_down = (
        jnp.einsum("lsh,lsd->lhd", hidden, cot_full, preferred_element_type=jnp.float32) * inv_count
    ).astype(jnp.bfloat16)
    grad_gate = (
        jnp.einsum("lsd,lsh->ldh", expert_in, d_gate, preferred_element_type=jnp.float32)
        * inv_count
    ).astype(jnp.bfloat16)
    grad_up = (
        jnp.einsum("lsd,lsh->ldh", expert_in, d_up, preferred_element_type=jnp.float32) * inv_count
    ).astype(jnp.bfloat16)
    running = jnp.einsum(
        "lsh,lch->lsc",
        lax.all_gather(d_gate, "expert", axis=2, tiled=True),
        gate_rows,
        preferred_element_type=jnp.float32,
    )
    d_rows = (
        running
        + jnp.einsum(
            "lsh,lch->lsc",
            lax.all_gather(d_up, "expert", axis=2, tiled=True),
            up_rows,
            preferred_element_type=jnp.float32,
        )
    ).astype(jnp.bfloat16)
    grad_back = lax.all_to_all(
        from_experts(d_rows, dp_size), "dp", split_axis=0, concat_axis=0, tiled=True
    )
    input_grad = combine(grad_back, dest_index, keep_float, tok_rows, top_count).astype(
        jnp.bfloat16
    )
    return (output, input_grad, grad_gate, grad_up, grad_down)


def swap(values, axis_name, bit):
    size = lax.axis_size(axis_name)
    return lax.ppermute(values, axis_name, [(i, i ^ bit) for i in range(size)])


def shift(values, steps):
    size = lax.axis_size("dp")
    return lax.ppermute(values, "dp", [(i, (i + 4 * steps) % size) for i in range(size)])


def own_half(values):
    rows = values.shape[0] // 2
    return lax.dynamic_slice_in_dim(values, lax.axis_index("expert") * rows, rows, 0)


def gather_line(block, line):
    pieces = []
    current = block
    for step in range(line):
        following = shift(current, 1) if step < line - 1 else None
        from_x = swap(own_half(current), "dp", 2)
        from_y = swap(from_x, "expert", 1)
        mine = (current, from_x, from_y)
        pieces.append(mine + tuple(swap(piece, "dp", 1) for piece in mine))
        current = following
    return pieces


def gather_small(values, line):
    pair = jnp.stack([values, swap(values, "dp", 1)])
    quad = jnp.stack([pair, swap(pair, "dp", 2)])
    return jnp.stack([quad] + [shift(quad, step) for step in range(1, line)])


def add_bf16(a, b):
    return (a.astype(jnp.float32) + b.astype(jnp.float32)).astype(jnp.bfloat16)


def send_home(keep, send, step):
    axes = (("dp", 2), ("expert", 1)) if step % 2 == 0 else (("expert", 1), ("dp", 2))
    got = swap(send, "dp", 1)
    away = swap(add_bf16(keep[1], got[1]), *axes[0])
    home = add_bf16(keep[0], got[0])
    last = swap(add_bf16(home[1], away[1]), *axes[1])
    total = add_bf16(add_bf16(home[0], away[0]), last)
    return shift(total, -step) if step else total


def mxu(a, b, dims=((1,), (0,))):
    return lax.dot_general(a, b, (dims, ((), ())), preferred_element_type=jnp.float32)


def take_rows(pick_ref, pieces, store):
    for x in range(2):
        for core in range(2):
            own, half_a, half_b = pieces[3 * core : 3 * core + 3]
            if x == 0:
                block = own[...]
            else:
                block = jnp.concatenate([half_a[...], half_b[...]], axis=0)
            store(2 * x + core, mxu(pick_ref[x, core], block))


def spread_rows(step, part, half, rows, place_ref, keep_ref, send_ref):
    capacity = rows.shape[0] // 4
    side = half ^ part
    for x in range(2):
        for core in range(2):
            group = 2 * x + core
            piece = rows[group * capacity : (group + 1) * capacity]
            out = mxu(place_ref[x, core], piece).astype(jnp.bfloat16)
            target = keep_ref if core == 0 else send_ref
            if step % 2 == 0:
                target[x, side] = out
            else:
                target[side, x] = out


def forward_kernel(step, part_ref, pick_ref, place_ref, scale_ref, *refs):
    pieces, refs = refs[:6], refs[6:]
    w_gate, w_up, w_down, rows_ref, gate_ref, up_ref, hidden_ref, keep_ref, send_ref = refs
    capacity = pick_ref.shape[2]

    def store(group, rows):
        rows_ref[pl.ds(group * capacity, capacity), :] = rows.astype(jnp.bfloat16)

    take_rows(pick_ref, pieces, store)
    expert_in = rows_ref[...]
    gate_val = mxu(expert_in, w_gate[...])
    up_val = mxu(expert_in, w_up[...])
    gate_ref[...] = gate_val
    up_ref[...] = up_val
    hidden = (gate_val * jax.nn.sigmoid(gate_val) * up_val).astype(jnp.bfloat16)
    hidden_ref[...] = hidden
    width = w_down.shape[1] // 2
    for half in range(2):
        out = mxu(hidden, w_down[:, half * width : (half + 1) * width])
        out = (out * scale_ref[...]).astype(jnp.bfloat16)
        spread_rows(step, part_ref[0], half, out, place_ref, keep_ref, send_ref)


def backward_kernel(step, part_ref, pick_ref, place_ref, scale_ref, *refs):
    pieces, refs = refs[:6], refs[6:]
    gate_ref, up_ref, w_gate, w_up, w_down = refs[:5]
    rows_ref, d_gate_ref, d_up_ref, keep_ref, send_ref = refs[5:]
    capacity = pick_ref.shape[2]

    def store(group, rows):
        span = pl.ds(group * capacity, capacity)
        rows_ref[span, :] = (rows * scale_ref[span, :]).astype(jnp.bfloat16)

    take_rows(pick_ref, pieces, store)
    d_hidden = mxu(rows_ref[...], w_down[...], ((1,), (1,)))
    act_val, act_slope = silu_parts(gate_ref[...])
    d_gate = (d_hidden * up_ref[...] * act_slope).astype(jnp.bfloat16)
    d_up = (d_hidden * act_val).astype(jnp.bfloat16)
    d_gate_ref[...] = d_gate
    d_up_ref[...] = d_up
    width = w_gate.shape[0] // 2
    for half in range(2):
        span = slice(half * width, (half + 1) * width)
        out = mxu(d_gate, w_gate[span, :], ((1,), (1,))) + mxu(d_up, w_up[span, :], ((1,), (1,)))
        spread_rows(
            step, part_ref[0], half, out.astype(jnp.bfloat16), place_ref, keep_ref, send_ref
        )


def call_kernel(kernel, name, shapes, flops, args):
    space = pl.BlockSpec(memory_space=pltpu.VMEM)
    moved = sum(math.prod(a.shape) * a.dtype.itemsize for a in args + shapes)
    return pl.pallas_call(
        kernel,
        out_shape=shapes,
        in_specs=[pl.BlockSpec(memory_space=pltpu.SMEM)] + [space] * (len(args) - 1),
        out_specs=[space] * len(shapes),
        compiler_params=pltpu.CompilerParams(vmem_limit_bytes=40 * 2**20),
        cost_estimate=pl.CostEstimate(flops=flops, bytes_accessed=moved, transcendentals=0),
        name=name,
    )(*args)


def dense_plan(tokens, routes, kept_mask, gate_probs, output_grad, w_gate, w_up, w_down):
    dp_size = lax.axis_size("dp")
    line = dp_size // 4
    tok_rows, top_count = routes.shape
    capacity = tok_rows * top_count // dp_size
    model_width = tokens.shape[1]
    hidden_part = w_gate.shape[2]
    rows = 4 * capacity
    part = lax.axis_index("expert")
    w_gate, w_up, w_down = w_gate[0], w_up[0], w_down[0]

    table = jnp.concatenate(
        [routes.T.astype(jnp.float32), kept_mask.T.astype(jnp.float32), gate_probs.T], axis=0
    )
    table = gather_small(table, line)
    chosen, kept, probs = jnp.split(table, 3, axis=3)
    expert = lax.axis_index("dp").astype(jnp.float32)
    hit = jnp.where(chosen == expert, kept, 0.0)
    used = jnp.sum(hit, axis=3)
    weight = jnp.sum(hit * probs, axis=3)
    kept_count = jnp.sum(used)
    earlier = jnp.triu(jnp.ones((tok_rows, tok_rows), jnp.bfloat16), 1)
    rank = jnp.einsum(
        "sabt,tu->sabu", used.astype(jnp.bfloat16), earlier, preferred_element_type=jnp.float32
    )
    slots = jnp.arange(capacity, dtype=jnp.float32)[:, None]
    pick = jnp.where(rank[..., None, :] == slots, used[..., None, :], 0.0)
    row_weight = jnp.sum(pick * weight[..., None, :], axis=4).reshape(line, rows, 1)
    pick = pick.astype(jnp.bfloat16)
    place = jnp.swapaxes(pick, 3, 4)
    turned = jnp.where(part == 0, pick[:, 1], jnp.roll(pick[:, 1], tok_rows // 2, axis=3))
    pick_in = jnp.stack([pick[:, 0], turned], axis=1)

    token_pieces = gather_line(tokens, line)
    cot_pieces = gather_line(output_grad, line)

    def array(shape, dtype=jnp.bfloat16):
        return jax.ShapeDtypeStruct(shape, dtype)

    wide = array((rows, model_width))
    narrow, narrow_float = array((rows, hidden_part)), array((rows, hidden_part), jnp.float32)
    home = array((2, 2, tok_rows, model_width // 2))
    flops = 6 * rows * model_width * hidden_part
    part_arg = part.astype(jnp.int32).reshape(1)
    saved, outputs, grads, finals = [], [], [], []
    for step in range(line):
        expert_in, gate_val, up_val, hidden, keep, send = call_kernel(
            functools.partial(forward_kernel, step),
            "forward_chunk",
            [wide, narrow_float, narrow_float, narrow, home, home],
            flops,
            [part_arg, pick_in[step], place[step], row_weight[step], *token_pieces[step]]
            + [w_gate, w_up, w_down],
        )
        outputs.append(send_home(keep, send, step))
        saved.append((expert_in, gate_val, up_val, hidden))
    for step in range(line):
        expert_in, gate_val, up_val, hidden = saved[step]
        cot_rows, d_gate, d_up, keep, send = call_kernel(
            functools.partial(backward_kernel, step),
            "backward_chunk",
            [wide, narrow, narrow, home, home],
            flops,
            [part_arg, pick_in[step], place[step], row_weight[step], *cot_pieces[step]]
            + [gate_val, up_val, w_gate, w_up, w_down],
        )
        grads.append(send_home(keep, send, step))
        finals.append((expert_in, hidden, cot_rows, d_gate, d_up))
    expert_in, hidden, cot_rows, d_gate, d_up = (
        jnp.concatenate(parts, axis=0) for parts in zip(*finals)
    )
    inv_count = 1.0 / jnp.maximum(kept_count, 1.0)
    by_row = ((0,), (0,))
    grad_down = (mxu(hidden, cot_rows, by_row) * inv_count).astype(jnp.bfloat16)
    grad_gate = (mxu(expert_in, d_gate, by_row) * inv_count).astype(jnp.bfloat16)
    grad_up = (mxu(expert_in, d_up, by_row) * inv_count).astype(jnp.bfloat16)
    output = sum(part_sum.astype(jnp.float32) for part_sum in outputs).astype(jnp.bfloat16)
    input_grad = sum(part_sum.astype(jnp.float32) for part_sum in grads).astype(jnp.bfloat16)
    return (output, input_grad, grad_gate[None], grad_up[None], grad_down[None])


def per_device(tokens, routes, kept_mask, gate_probs, output_grad, w_gate, w_up, w_down):
    dp_size = lax.axis_size("dp")
    local_experts = w_gate.shape[0]
    top_count = routes.shape[1]
    dense = (
        local_experts == 1
        and lax.axis_size("expert") == 2
        and dp_size % 4 == 0
        and 2 * top_count >= dp_size
    )
    plan = dense_plan if dense else routed_plan
    return plan(tokens, routes, kept_mask, gate_probs, output_grad, w_gate, w_up, w_down)


def solution(mesh):
    placed = (
        P("dp", None),
        P("dp", None),
        P("dp", None),
        P("dp", None),
        P("dp", None),
        P("dp", None, "expert"),
        P("dp", None, "expert"),
        P("dp", "expert", None),
    )
    return jax.shard_map(
        per_device,
        mesh=mesh,
        in_specs=placed,
        out_specs=(
            P("dp", "expert"),
            P("dp", "expert"),
            P("dp", None, "expert"),
            P("dp", None, "expert"),
            P("dp", "expert", None),
        ),
        check_vma=False,
    )
```

```python
import functools
import math

import jax
import jax.numpy as jnp
from jax import lax
from jax.experimental import pallas as pl
from jax.experimental.pallas import tpu as pltpu
from jax.sharding import PartitionSpec as P


def silu_parts(gate_val):
    sigmoid_val = jax.nn.sigmoid(gate_val)
    return (gate_val * sigmoid_val, sigmoid_val * (1.0 + gate_val * (1.0 - sigmoid_val)))


def slot_layout(routes, experts):
    tok_rows, top_count = routes.shape
    pair_count = tok_rows * top_count
    flat_routes = routes.reshape(pair_count)
    onehot = (flat_routes[:, None] == jnp.arange(experts, dtype=jnp.int32)[None, :]).astype(
        jnp.int32
    )
    before = jnp.cumsum(onehot, axis=0) - onehot
    slot_index = jnp.sum(before * onehot, axis=1)
    capacity = pair_count // experts
    dest_index = flat_routes * capacity + slot_index
    source = (
        jnp.zeros((pair_count,), jnp.int32)
        .at[dest_index]
        .set(jnp.arange(pair_count, dtype=jnp.int32))
    )
    return (dest_index, source, onehot)


def to_experts(rows_in, dp_size, local_experts):
    capacity = rows_in.shape[1]
    width = rows_in.shape[2]
    grouped = rows_in.reshape(dp_size, local_experts, capacity, width)
    return jnp.swapaxes(grouped, 0, 1).reshape(local_experts, dp_size * capacity, width)


def from_experts(values, dp_size):
    local_experts, slot_total, width = values.shape
    capacity = slot_total // dp_size
    grouped = values.reshape(local_experts, dp_size, capacity, width)
    return jnp.swapaxes(grouped, 0, 1).reshape(dp_size * local_experts, capacity, width)


def combine(back_rows, dest_index, factor, tok_rows, top_count):
    width = back_rows.shape[2]
    picked = back_rows.reshape(-1, width)[dest_index].astype(jnp.float32) * factor[:, None]
    return jnp.sum(picked.reshape(tok_rows, top_count, width), axis=1)


def routed_plan(tokens, routes, kept_mask, gate_probs, output_grad, w_gate, w_up, w_down):
    dp_size = lax.axis_size("dp")
    part_count = lax.axis_size("expert")
    local_experts, model_width, hidden_part = w_gate.shape
    experts = local_experts * dp_size
    tok_rows, top_count = routes.shape
    capacity = tok_rows * top_count // experts
    col_width = model_width // part_count
    dest_index, source, onehot = slot_layout(routes, experts)
    keep_float = kept_mask.reshape(-1).astype(jnp.float32)
    weight_flat = keep_float * gate_probs.reshape(-1)
    src_token = source // top_count
    src_keep = keep_float[source]
    src_weight = weight_flat[source]
    col_start = lax.axis_index("expert") * col_width
    token_src = lax.dynamic_slice_in_dim(tokens, col_start, col_width, 1)
    cot_src = lax.dynamic_slice_in_dim(output_grad, col_start, col_width, 1)
    send_width = token_src.shape[1]
    rows_send = (token_src[src_token].astype(jnp.float32) * src_keep[:, None]).astype(jnp.bfloat16)
    rows_send = rows_send.reshape(experts, capacity, send_width)
    cot_send = (cot_src[src_token].astype(jnp.float32) * src_weight[:, None]).astype(jnp.bfloat16)
    cot_send = cot_send.reshape(experts, capacity, send_width)
    totals = jnp.sum(onehot.astype(jnp.float32) * keep_float[:, None], axis=0)
    totals = lax.psum(totals, "dp")
    kept_count = lax.dynamic_slice_in_dim(
        totals, lax.axis_index("dp") * local_experts, local_experts
    )
    rows_in = lax.all_to_all(rows_send, "dp", split_axis=0, concat_axis=0, tiled=True)
    cot_in = lax.all_to_all(cot_send, "dp", split_axis=0, concat_axis=0, tiled=True)
    rows_in = lax.all_gather(rows_in, "expert", axis=2, tiled=True)
    cot_in = lax.all_gather(cot_in, "expert", axis=2, tiled=True)
    expert_in = to_experts(rows_in, dp_size, local_experts)
    cot_full = to_experts(cot_in, dp_size, local_experts)
    down_cols = lax.all_to_all(w_down, "expert", split_axis=2, concat_axis=1, tiled=True)
    gate_rows, up_rows = (
        lax.all_to_all(w_gate, "expert", split_axis=1, concat_axis=2, tiled=True),
        lax.all_to_all(w_up, "expert", split_axis=1, concat_axis=2, tiled=True),
    )
    gate_val = jnp.einsum("lsd,ldh->lsh", expert_in, w_gate, preferred_element_type=jnp.float32)
    up_val = jnp.einsum("lsd,ldh->lsh", expert_in, w_up, preferred_element_type=jnp.float32)
    act_val, act_slope = silu_parts(gate_val)
    hidden = (act_val * up_val).astype(jnp.bfloat16)
    expert_out = jnp.einsum(
        "lsh,lhc->lsc",
        lax.all_gather(hidden, "expert", axis=2, tiled=True),
        down_cols,
        preferred_element_type=jnp.float32,
    ).astype(jnp.bfloat16)
    out_back = lax.all_to_all(
        from_experts(expert_out, dp_size), "dp", split_axis=0, concat_axis=0, tiled=True
    )
    output = combine(out_back, dest_index, weight_flat, tok_rows, top_count).astype(jnp.bfloat16)
    d_hidden = jnp.einsum("lsd,lhd->lsh", cot_full, w_down, preferred_element_type=jnp.float32)
    d_gate = (d_hidden * up_val * act_slope).astype(jnp.bfloat16)
    d_up = (d_hidden * act_val).astype(jnp.bfloat16)
    inv_count = (1.0 / jnp.maximum(kept_count, 1.0))[:, None, None]
    grad_down = (
        jnp.einsum("lsh,lsd->lhd", hidden, cot_full, preferred_element_type=jnp.float32) * inv_count
    ).astype(jnp.bfloat16)
    grad_gate = (
        jnp.einsum("lsd,lsh->ldh", expert_in, d_gate, preferred_element_type=jnp.float32)
        * inv_count
    ).astype(jnp.bfloat16)
    grad_up = (
        jnp.einsum("lsd,lsh->ldh", expert_in, d_up, preferred_element_type=jnp.float32) * inv_count
    ).astype(jnp.bfloat16)
    running = jnp.einsum(
        "lsh,lch->lsc",
        lax.all_gather(d_gate, "expert", axis=2, tiled=True),
        gate_rows,
        preferred_element_type=jnp.float32,
    )
    d_rows = (
        running
        + jnp.einsum(
            "lsh,lch->lsc",
            lax.all_gather(d_up, "expert", axis=2, tiled=True),
            up_rows,
            preferred_element_type=jnp.float32,
        )
    ).astype(jnp.bfloat16)
    grad_back = lax.all_to_all(
        from_experts(d_rows, dp_size), "dp", split_axis=0, concat_axis=0, tiled=True
    )
    input_grad = combine(grad_back, dest_index, keep_float, tok_rows, top_count).astype(
        jnp.bfloat16
    )
    return (output, input_grad, grad_gate, grad_up, grad_down)


def swap(values, axis_name, bit):
    size = lax.axis_size(axis_name)
    return lax.ppermute(values, axis_name, [(i, i ^ bit) for i in range(size)])


def shift(values, steps):
    size = lax.axis_size("dp")
    return lax.ppermute(values, "dp", [(i, (i + 4 * steps) % size) for i in range(size)])


def cut_halves(part_ref, tokens, cots, mine, other):
    rows = tokens.shape[0] // 2
    own = pl.multiple_of(part_ref[0] * rows, rows)
    rest = pl.multiple_of(rows - part_ref[0] * rows, rows)
    for kind, values in enumerate((tokens, cots)):
        mine[kind] = values[pl.ds(own, rows), :]
        other[kind] = values[pl.ds(rest, rows), :]


def own_halves(part_arg, tokens, cots):
    shape = jax.ShapeDtypeStruct((2, tokens.shape[0] // 2, tokens.shape[1]), tokens.dtype)
    vmem = pl.BlockSpec(memory_space=pltpu.VMEM)
    return call_kernel(
        cut_halves,
        "own_halves",
        [shape, shape],
        [part_arg, tokens, cots],
        in_specs=[pl.BlockSpec(memory_space=pltpu.SMEM), vmem, vmem],
    )


def gather_line(part_arg, tokens, cots, line):
    mine, other = own_halves(part_arg, tokens, cots)
    halves = [mine]
    for _ in range(line - 1):
        halves.append(shift(halves[-1], 1))
    steps = []
    for step, half in enumerate(halves):
        rest = swap(half, "expert", 1) if step else other
        across = swap(half, "dp", 2)
        if step:
            last = (swap(rest[0], "dp", 2), swap(across[1], "expert", 1))
        else:
            last = tuple(swap(across[kind], "expert", 1) for kind in range(2))
        pieces = (half, rest, across) + last
        steps.append(pieces + tuple(swap(piece, "dp", 1) for piece in pieces))
    return steps


def gather_small(values, line):
    lines = jnp.stack([values] + [shift(values, step) for step in range(1, line)])
    pairs = jnp.stack([lines, swap(lines, "dp", 2)], axis=1)
    return jnp.stack([pairs, swap(pairs, "dp", 1)], axis=2)


def mxu(a, b, dims=((1,), (0,))):
    return lax.dot_general(a, b, (dims, ((), ())), preferred_element_type=jnp.float32)


def add_to(target, *terms):
    target[...] = sum(term.astype(jnp.float32) for term in terms).astype(jnp.bfloat16)


def add_cores(keep, got, *refs):
    away_out, away_grad, home = refs
    add_to(away_out, keep[0, 1], got[0, 1])
    add_to(away_grad, keep[1, 1], got[1, 1])
    add_to(home, keep[:, 0], got[:, 0])


def add_first(home, away_out, away_grad, *refs):
    last_out, last_grad = refs[-2:]
    add_to(last_out, home[0, 1], away_out[1])
    add_to(last_grad, home[1, 1], away_grad[1])


def add_last(home, away_out, away_grad, last_out, last_grad, *refs):
    total = refs[-1]
    add_to(total.at[0], home[0, 0], away_out[0], last_out[...])
    add_to(total.at[1], home[1, 0], away_grad[0], last_grad[...])


def call_kernel(kernel, name, shapes, args, flops=0, vmem=8 * 2**20, **options):
    space = pl.BlockSpec(memory_space=pltpu.VMEM)
    moved = sum(math.prod(a.shape) * a.dtype.itemsize for a in [*args, *shapes])
    return pl.pallas_call(
        kernel,
        out_shape=shapes,
        in_specs=options.pop("in_specs", [space] * len(args)),
        out_specs=options.pop("out_specs", [space] * len(shapes)),
        compiler_params=pltpu.CompilerParams(vmem_limit_bytes=vmem),
        cost_estimate=pl.CostEstimate(flops=flops, bytes_accessed=moved, transcendentals=0),
        name=name,
        **options,
    )(*args)


def send_home(keep, send, step):
    def array(*shape):
        return jax.ShapeDtypeStruct(shape, jnp.bfloat16)

    rows, columns = keep.shape[3:]
    pair, single = array(2, rows, columns), array(rows, columns)
    got = swap(send, "dp", 1)
    away_out, away_grad, home = call_kernel(
        add_cores, "add_cores", [pair, pair, array(2, 2, rows, columns)], [keep, got]
    )
    away = (swap(away_out, "dp", 2), swap(away_grad, "expert", 1))
    lasts = call_kernel(add_first, "add_first", [single, single], [home, *away])
    last = (swap(lasts[0], "expert", 1), swap(lasts[1], "dp", 2))
    total = call_kernel(add_last, "add_last", [pair], [home, *away, *last])[0]
    return shift(total, -step) if step else total


def take_rows(kind, pick_ref, pieces, store):
    for x in range(2):
        for core in range(2):
            half, rest, across, *last = pieces[5 * core : 5 * core + 5]
            if x == 0:
                block = jnp.concatenate([half[kind], rest[kind]], axis=0)
            else:
                block = jnp.concatenate([across[kind], last[kind][...]], axis=0)
            store(2 * x + core, mxu(pick_ref[x, core], block))


def spread_rows(kind, part, half, rows, place_ref, keep_ref, send_ref):
    capacity = rows.shape[0] // 4
    side = half ^ part
    for x in range(2):
        for core in range(2):
            group = 2 * x + core
            piece = rows[group * capacity : (group + 1) * capacity]
            out = mxu(place_ref[x, core], piece).astype(jnp.bfloat16)
            target = keep_ref if core == 0 else send_ref
            if kind == 0:
                target[kind, x, side] = out
            else:
                target[kind, side, x] = out


def chunk_kernel(step, part_ref, pick_ref, place_ref, scale_ref, *refs):
    sources, refs = refs[:13], refs[-30:]
    outs, saved = refs[:2], refs[2:7]
    kept, buffers, homes, sems = refs[7:12], refs[12:25], refs[25:27], refs[27:]
    keep_ref, send_ref = homes
    rows_ref, cot_ref, hidden_ref, d_gate_ref, d_up_ref = kept
    pieces, (w_gate, w_up, w_down) = buffers[:10], buffers[10:]
    rows, capacity = rows_ref.shape[0], pick_ref.shape[2]
    loads = [
        pltpu.make_async_copy(source, target, sems[0].at[i])
        for i, (source, target) in enumerate(zip(sources, buffers))
    ]
    stores = [
        pltpu.make_async_copy(source, target.at[pl.ds(step * rows, rows)], sems[1].at[i])
        for i, (source, target) in enumerate(zip(kept, saved))
    ]
    sends = [
        pltpu.make_async_copy(source.at[kind], target.at[kind], sems[2].at[kind, i])
        for kind in range(2)
        for i, (source, target) in enumerate(zip(homes, outs))
    ]
    for load in loads:
        load.start()

    def store_rows(group, found):
        rows_ref[pl.ds(group * capacity, capacity), :] = found.astype(jnp.bfloat16)

    def store_cot(group, found):
        span = pl.ds(group * capacity, capacity)
        cot_ref[span, :] = (found * scale_ref[span, :]).astype(jnp.bfloat16)

    for load in loads[:10]:
        load.wait()
    take_rows(0, pick_ref, pieces, store_rows)
    stores[0].start()
    take_rows(1, pick_ref, pieces, store_cot)
    stores[1].start()
    for load in loads[10:]:
        load.wait()
    expert_in = rows_ref[...]
    gate_val = mxu(expert_in, w_gate[...])
    up_val = mxu(expert_in, w_up[...])
    act_val, act_slope = silu_parts(gate_val)
    hidden = (act_val * up_val).astype(jnp.bfloat16)
    hidden_ref[...] = hidden
    stores[2].start()
    d_hidden = mxu(cot_ref[...], w_down[...], ((1,), (1,)))
    d_gate = (d_hidden * up_val * act_slope).astype(jnp.bfloat16)
    d_up = (d_hidden * act_val).astype(jnp.bfloat16)
    d_gate_ref[...] = d_gate
    d_up_ref[...] = d_up
    stores[3].start()
    stores[4].start()
    width = w_down.shape[1] // 2
    part = part_ref[0]
    halves = [slice(half * width, (half + 1) * width) for half in range(2)]
    for half, span in enumerate(halves):
        out = (mxu(hidden, w_down[:, span]) * scale_ref[...]).astype(jnp.bfloat16)
        spread_rows(0, part, half, out, place_ref, keep_ref, send_ref)
    for send in sends[:2]:
        send.start()
    for half, span in enumerate(halves):
        grad = mxu(d_gate, w_gate[span, :], ((1,), (1,))) + mxu(d_up, w_up[span, :], ((1,), (1,)))
        spread_rows(1, part, half, grad.astype(jnp.bfloat16), place_ref, keep_ref, send_ref)
    for send in sends[2:]:
        send.start()
    for copy in stores + sends:
        copy.wait()


def run_chunk(step, tables, sources, saved_shapes, saved):
    def array(a):
        return jax.ShapeDtypeStruct(a.shape, a.dtype)

    def scratch(a):
        return pltpu.VMEM(a.shape, a.dtype)

    kinds, half_rows, model_width = sources[0].shape
    home = jax.ShapeDtypeStruct((kinds, 2, 2, 2 * half_rows, model_width // 2), jnp.bfloat16)
    vmem, hbm = pl.BlockSpec(memory_space=pltpu.VMEM), pl.BlockSpec(memory_space=pl.ANY)
    rows = tables[-1].shape[0]
    first_saved = len(tables) + len(sources)
    return call_kernel(
        functools.partial(chunk_kernel, step),
        "chunk",
        [home, home, *saved_shapes],
        [*tables, *sources, *saved],
        vmem=60 * 2**20,
        flops=12 * rows * sources[-1].shape[0] * sources[-1].shape[1],
        in_specs=[pl.BlockSpec(memory_space=pltpu.SMEM)]
        + [vmem] * (len(tables) - 1)
        + [hbm] * (len(sources) + len(saved)),
        out_specs=[hbm] * (2 + len(saved_shapes)),
        input_output_aliases={first_saved + i: 2 + i for i in range(len(saved))},
        scratch_shapes=[pltpu.VMEM((rows, s.shape[1]), s.dtype) for s in saved_shapes]
        + [scratch(source) for source in sources]
        + [scratch(home)] * 2
        + [pltpu.SemaphoreType.DMA(n) for n in ((len(sources),), (len(saved_shapes),), (2, 2))],
    )


def dense_plan(tokens, routes, kept_mask, gate_probs, output_grad, w_gate, w_up, w_down):
    dp_size = lax.axis_size("dp")
    line = dp_size // 4
    tok_rows, top_count = routes.shape
    capacity = tok_rows * top_count // dp_size
    model_width = tokens.shape[1]
    hidden_part = w_gate.shape[2]
    rows = 4 * capacity
    part = lax.axis_index("expert")
    w_gate, w_up, w_down = w_gate[0], w_up[0], w_down[0]

    table = jnp.concatenate(
        [routes.T.astype(jnp.float32), kept_mask.T.astype(jnp.float32), gate_probs.T], axis=0
    )
    table = gather_small(table, line)
    chosen, kept, probs = jnp.split(table, 3, axis=3)
    expert = lax.axis_index("dp").astype(jnp.float32)
    hit = jnp.where(chosen == expert, kept, 0.0)
    used = jnp.sum(hit, axis=3)
    weight = jnp.sum(hit * probs, axis=3)
    kept_count = jnp.sum(used)
    earlier = jnp.triu(jnp.ones((tok_rows, tok_rows), jnp.bfloat16), 1)
    rank = jnp.einsum(
        "sabt,tu->sabu", used.astype(jnp.bfloat16), earlier, preferred_element_type=jnp.float32
    )
    slots = jnp.arange(capacity, dtype=jnp.float32)[:, None]
    pick = jnp.where(rank[..., None, :] == slots, used[..., None, :], 0.0)
    row_weight = jnp.sum(pick * weight[..., None, :], axis=4).reshape(line, rows, 1)
    pick = pick.astype(jnp.bfloat16)
    place = jnp.swapaxes(pick, 3, 4)
    pick_in = jnp.where(part == 0, pick, jnp.roll(pick, tok_rows // 2, axis=4))

    part_arg = part.astype(jnp.int32).reshape(1)
    pieces = gather_line(part_arg, tokens, output_grad, line)

    def saved_array(width):
        return jax.ShapeDtypeStruct((line * rows, width), jnp.bfloat16)

    saved_shapes = [saved_array(model_width)] * 2 + [saved_array(hidden_part)] * 3
    saved, returns = [], []

    for step in range(line):
        keep, send, *saved = run_chunk(
            step,
            [part_arg, pick_in[step], place[step], row_weight[step]],
            [*pieces[step], w_gate, w_up, w_down],
            saved_shapes,
            saved,
        )
        returns.append(send_home(keep, send, step))
    expert_in, cot_rows, hidden, d_gate, d_up = saved
    inv_count = 1.0 / jnp.maximum(kept_count, 1.0)
    by_row = ((0,), (0,))
    grad_down = (mxu(hidden, cot_rows, by_row) * inv_count).astype(jnp.bfloat16)
    grad_gate = (mxu(expert_in, d_gate, by_row) * inv_count).astype(jnp.bfloat16)
    grad_up = (mxu(expert_in, d_up, by_row) * inv_count).astype(jnp.bfloat16)
    results = sum(part_sum.astype(jnp.float32) for part_sum in returns).astype(jnp.bfloat16)
    return (results[0], results[1], grad_gate[None], grad_up[None], grad_down[None])


def per_device(tokens, routes, kept_mask, gate_probs, output_grad, w_gate, w_up, w_down):
    dp_size = lax.axis_size("dp")
    local_experts = w_gate.shape[0]
    top_count = routes.shape[1]
    dense = (
        local_experts == 1
        and lax.axis_size("expert") == 2
        and dp_size % 4 == 0
        and 2 * top_count >= dp_size
    )
    plan = dense_plan if dense else routed_plan
    return plan(tokens, routes, kept_mask, gate_probs, output_grad, w_gate, w_up, w_down)


def solution(mesh):
    placed = (
        P("dp", None),
        P("dp", None),
        P("dp", None),
        P("dp", None),
        P("dp", None),
        P("dp", None, "expert"),
        P("dp", None, "expert"),
        P("dp", "expert", None),
    )
    return jax.shard_map(
        per_device,
        mesh=mesh,
        in_specs=placed,
        out_specs=(
            P("dp", "expert"),
            P("dp", "expert"),
            P("dp", None, "expert"),
            P("dp", None, "expert"),
            P("dp", "expert", None),
        ),
        check_vma=False,
    )
```

```python
import functools
import math

import jax
import jax.numpy as jnp
from jax import lax
from jax.experimental import pallas as pl
from jax.experimental.pallas import tpu as pltpu
from jax.sharding import PartitionSpec as P


def silu_parts(gate_val):
    sigmoid_val = jax.nn.sigmoid(gate_val)
    return (gate_val * sigmoid_val, sigmoid_val * (1.0 + gate_val * (1.0 - sigmoid_val)))


def slot_layout(routes, experts):
    tok_rows, top_count = routes.shape
    pair_count = tok_rows * top_count
    flat_routes = routes.reshape(pair_count)
    onehot = (flat_routes[:, None] == jnp.arange(experts, dtype=jnp.int32)[None, :]).astype(
        jnp.int32
    )
    before = jnp.cumsum(onehot, axis=0) - onehot
    slot_index = jnp.sum(before * onehot, axis=1)
    capacity = pair_count // experts
    dest_index = flat_routes * capacity + slot_index
    source = (
        jnp.zeros((pair_count,), jnp.int32)
        .at[dest_index]
        .set(jnp.arange(pair_count, dtype=jnp.int32))
    )
    return (dest_index, source, onehot)


def to_experts(rows_in, dp_size, local_experts):
    capacity = rows_in.shape[1]
    width = rows_in.shape[2]
    grouped = rows_in.reshape(dp_size, local_experts, capacity, width)
    return jnp.swapaxes(grouped, 0, 1).reshape(local_experts, dp_size * capacity, width)


def from_experts(values, dp_size):
    local_experts, slot_total, width = values.shape
    capacity = slot_total // dp_size
    grouped = values.reshape(local_experts, dp_size, capacity, width)
    return jnp.swapaxes(grouped, 0, 1).reshape(dp_size * local_experts, capacity, width)


def combine(back_rows, dest_index, factor, tok_rows, top_count):
    width = back_rows.shape[2]
    picked = back_rows.reshape(-1, width)[dest_index].astype(jnp.float32) * factor[:, None]
    return jnp.sum(picked.reshape(tok_rows, top_count, width), axis=1)


def routed_plan(tokens, routes, kept_mask, gate_probs, output_grad, w_gate, w_up, w_down):
    dp_size = lax.axis_size("dp")
    part_count = lax.axis_size("expert")
    local_experts, model_width, hidden_part = w_gate.shape
    experts = local_experts * dp_size
    tok_rows, top_count = routes.shape
    capacity = tok_rows * top_count // experts
    col_width = model_width // part_count
    dest_index, source, onehot = slot_layout(routes, experts)
    keep_float = kept_mask.reshape(-1).astype(jnp.float32)
    weight_flat = keep_float * gate_probs.reshape(-1)
    src_token = source // top_count
    src_keep = keep_float[source]
    src_weight = weight_flat[source]
    col_start = lax.axis_index("expert") * col_width
    token_src = lax.dynamic_slice_in_dim(tokens, col_start, col_width, 1)
    cot_src = lax.dynamic_slice_in_dim(output_grad, col_start, col_width, 1)
    send_width = token_src.shape[1]
    rows_send = (token_src[src_token].astype(jnp.float32) * src_keep[:, None]).astype(jnp.bfloat16)
    rows_send = rows_send.reshape(experts, capacity, send_width)
    cot_send = (cot_src[src_token].astype(jnp.float32) * src_weight[:, None]).astype(jnp.bfloat16)
    cot_send = cot_send.reshape(experts, capacity, send_width)
    totals = jnp.sum(onehot.astype(jnp.float32) * keep_float[:, None], axis=0)
    totals = lax.psum(totals, "dp")
    kept_count = lax.dynamic_slice_in_dim(
        totals, lax.axis_index("dp") * local_experts, local_experts
    )
    rows_in = lax.all_to_all(rows_send, "dp", split_axis=0, concat_axis=0, tiled=True)
    cot_in = lax.all_to_all(cot_send, "dp", split_axis=0, concat_axis=0, tiled=True)
    rows_in = lax.all_gather(rows_in, "expert", axis=2, tiled=True)
    cot_in = lax.all_gather(cot_in, "expert", axis=2, tiled=True)
    expert_in = to_experts(rows_in, dp_size, local_experts)
    cot_full = to_experts(cot_in, dp_size, local_experts)
    down_cols = lax.all_to_all(w_down, "expert", split_axis=2, concat_axis=1, tiled=True)
    gate_rows, up_rows = (
        lax.all_to_all(w_gate, "expert", split_axis=1, concat_axis=2, tiled=True),
        lax.all_to_all(w_up, "expert", split_axis=1, concat_axis=2, tiled=True),
    )
    gate_val = jnp.einsum("lsd,ldh->lsh", expert_in, w_gate, preferred_element_type=jnp.float32)
    up_val = jnp.einsum("lsd,ldh->lsh", expert_in, w_up, preferred_element_type=jnp.float32)
    act_val, act_slope = silu_parts(gate_val)
    hidden = (act_val * up_val).astype(jnp.bfloat16)
    expert_out = jnp.einsum(
        "lsh,lhc->lsc",
        lax.all_gather(hidden, "expert", axis=2, tiled=True),
        down_cols,
        preferred_element_type=jnp.float32,
    ).astype(jnp.bfloat16)
    out_back = lax.all_to_all(
        from_experts(expert_out, dp_size), "dp", split_axis=0, concat_axis=0, tiled=True
    )
    output = combine(out_back, dest_index, weight_flat, tok_rows, top_count).astype(jnp.bfloat16)
    d_hidden = jnp.einsum("lsd,lhd->lsh", cot_full, w_down, preferred_element_type=jnp.float32)
    d_gate = (d_hidden * up_val * act_slope).astype(jnp.bfloat16)
    d_up = (d_hidden * act_val).astype(jnp.bfloat16)
    inv_count = (1.0 / jnp.maximum(kept_count, 1.0))[:, None, None]
    grad_down = (
        jnp.einsum("lsh,lsd->lhd", hidden, cot_full, preferred_element_type=jnp.float32) * inv_count
    ).astype(jnp.bfloat16)
    grad_gate = (
        jnp.einsum("lsd,lsh->ldh", expert_in, d_gate, preferred_element_type=jnp.float32)
        * inv_count
    ).astype(jnp.bfloat16)
    grad_up = (
        jnp.einsum("lsd,lsh->ldh", expert_in, d_up, preferred_element_type=jnp.float32) * inv_count
    ).astype(jnp.bfloat16)
    running = jnp.einsum(
        "lsh,lch->lsc",
        lax.all_gather(d_gate, "expert", axis=2, tiled=True),
        gate_rows,
        preferred_element_type=jnp.float32,
    )
    d_rows = (
        running
        + jnp.einsum(
            "lsh,lch->lsc",
            lax.all_gather(d_up, "expert", axis=2, tiled=True),
            up_rows,
            preferred_element_type=jnp.float32,
        )
    ).astype(jnp.bfloat16)
    grad_back = lax.all_to_all(
        from_experts(d_rows, dp_size), "dp", split_axis=0, concat_axis=0, tiled=True
    )
    input_grad = combine(grad_back, dest_index, keep_float, tok_rows, top_count).astype(
        jnp.bfloat16
    )
    return (output, input_grad, grad_gate, grad_up, grad_down)


def swap(values, axis_name, bit):
    size = lax.axis_size(axis_name)
    return lax.ppermute(values, axis_name, [(i, i ^ bit) for i in range(size)])


def shift(values, steps):
    size = lax.axis_size("dp")
    return lax.ppermute(values, "dp", [(i, (i + 4 * steps) % size) for i in range(size)])


def cut_halves(part_ref, tokens, cots, table, mine, other, table_out):
    table_out[...] = table[...]
    rows = tokens.shape[0] // 2
    own = pl.multiple_of(part_ref[0] * rows, rows)
    rest = pl.multiple_of(rows - part_ref[0] * rows, rows)
    for kind, values in enumerate((tokens, cots)):
        mine[kind] = values[pl.ds(own, rows), :]
        other[kind] = values[pl.ds(rest, rows), :]


def own_halves(part_arg, tokens, cots, table):
    shape = jax.ShapeDtypeStruct((2, tokens.shape[0] // 2, tokens.shape[1]), tokens.dtype)
    vmem = pl.BlockSpec(memory_space=pltpu.VMEM)
    return call_kernel(
        cut_halves,
        "own_halves",
        [shape, shape, jax.ShapeDtypeStruct(table.shape, table.dtype)],
        [part_arg, tokens, cots, table],
        in_specs=[pl.BlockSpec(memory_space=pltpu.SMEM), vmem, vmem, vmem],
    )


def cut_kinds(rest, across, *refs):
    rest_out, across_out, mark, sems = refs[-4:]
    mark[...] = jnp.zeros_like(mark)
    copies = [
        pltpu.make_async_copy(rest.at[0], rest_out, sems.at[0]),
        pltpu.make_async_copy(across.at[1], across_out, sems.at[1]),
    ]
    for copy in copies:
        copy.start()
    for copy in copies:
        copy.wait()


def kinds_apart(rest, across, after):
    hbm = pl.BlockSpec(memory_space=pl.ANY)
    shape = jax.ShapeDtypeStruct(rest.shape[1:], rest.dtype)
    return call_kernel(
        cut_kinds,
        "cut_kinds",
        [shape, shape, jax.ShapeDtypeStruct((8, 128), jnp.float32)],
        [rest, across, *after],
        in_specs=[hbm] * (2 + len(after)),
        scratch_shapes=[pltpu.SemaphoreType.DMA((2,))],
    )


def gather_line(mine, other, line):
    halves = [mine]
    for _ in range(line - 1):
        halves.append(shift(halves[-1], 1))
    steps = []
    for step, half in enumerate(halves):
        rest = swap(half, "expert", 1) if step else other
        across = swap(half, "dp", 2)
        if step:
            tokens, cots, mark = kinds_apart(rest, across, ())
            last = (swap(tokens, "dp", 2), swap(cots, "expert", 1))
        else:
            last = (swap(across, "expert", 1),)
        pieces = (half, rest, across) + last
        steps.append(pieces + tuple(swap(piece, "dp", 1) for piece in pieces))
    return steps, mark


def gather_small(values, line):
    lines = jnp.stack([values] + [shift(values, step) for step in range(1, line)])
    pairs = jnp.stack([lines, swap(lines, "dp", 2)], axis=1)
    return jnp.stack([pairs, swap(pairs, "dp", 1)], axis=2)


def mxu(a, b, dims=((1,), (0,))):
    return lax.dot_general(a, b, (dims, ((), ())), preferred_element_type=jnp.float32)


def add_to(target, *terms):
    target[...] = sum(term.astype(jnp.float32) for term in terms).astype(jnp.bfloat16)


def add_cores(keep, got, *refs):
    away_out, away_grad, home, mark = refs[-4:]
    mark[...] = jnp.zeros_like(mark)
    add_to(away_out, keep[0, 1], got[0, 1])
    add_to(away_grad, keep[1, 1], got[1, 1])
    add_to(home, keep[:, 0], got[:, 0])


def add_first(home, away_out, away_grad, *refs):
    last_out, last_grad, mark = refs[-3:]
    mark[...] = jnp.zeros_like(mark)
    add_to(last_out, home[0, 1], away_out[1])
    add_to(last_grad, home[1, 1], away_grad[1])


def add_last(home, away_out, away_grad, last_out, last_grad, *refs):
    total, mark = refs[-2:]
    mark[...] = jnp.zeros_like(mark)
    add_to(total.at[0], home[0, 0], away_out[0], last_out[...])
    add_to(total.at[1], home[1, 0], away_grad[0], last_grad[...])


def call_kernel(kernel, name, shapes, args, flops=0, vmem=8 * 2**20, **options):
    space = pl.BlockSpec(memory_space=pltpu.VMEM)
    moved = sum(math.prod(a.shape) * a.dtype.itemsize for a in [*args, *shapes])
    return pl.pallas_call(
        kernel,
        out_shape=shapes,
        in_specs=options.pop("in_specs", [space] * len(args)),
        out_specs=options.pop("out_specs", [space] * len(shapes)),
        compiler_params=pltpu.CompilerParams(vmem_limit_bytes=vmem),
        cost_estimate=pl.CostEstimate(flops=flops, bytes_accessed=moved, transcendentals=0),
        name=name,
        **options,
    )(*args)


def send_home(keep, send, step, before):
    def array(*shape):
        return jax.ShapeDtypeStruct(shape, jnp.bfloat16)

    rows, columns = keep.shape[3:]
    pair, single = array(2, rows, columns), array(rows, columns)
    mark = jax.ShapeDtypeStruct((8, 128), jnp.float32)
    got = swap(send, "dp", 1)
    away_out, away_grad, home, mark_cores = call_kernel(
        add_cores, "add_cores", [pair, pair, array(2, 2, rows, columns), mark], [keep, got, *before[0]]
    )
    away = (swap(away_out, "dp", 2), swap(away_grad, "expert", 1))
    *lasts, mark_first = call_kernel(add_first, "add_first", [single, single, mark], [home, *away, *before[1]])
    last = (swap(lasts[0], "expert", 1), swap(lasts[1], "dp", 2))
    total, mark_last = call_kernel(add_last, "add_last", [pair, mark], [home, *away, *last, *before[2]])
    return shift(total, -step) if step else total, (mark_cores, mark_first, mark_last)


def take_rows(kind, pick_ref, pieces, store):
    for x in range(2):
        for core in range(2):
            half, rest, across, *last = pieces[core * len(pieces) // 2 : (core + 1) * len(pieces) // 2]
            if x == 0:
                block = jnp.concatenate([half[kind], rest[kind]], axis=0)
            else:
                rows = last[kind][...] if len(last) == 2 else last[0][kind]
                block = jnp.concatenate([across[kind], rows], axis=0)
            store(2 * x + core, mxu(pick_ref[x, core], block))


def spread_rows(kind, part, half, rows, place_ref, keep_ref, send_ref):
    capacity = rows.shape[0] // 4
    side = half ^ part
    for x in range(2):
        for core in range(2):
            group = 2 * x + core
            piece = rows[group * capacity : (group + 1) * capacity]
            out = mxu(place_ref[x, core], piece).astype(jnp.bfloat16)
            target = keep_ref if core == 0 else send_ref
            if kind == 0:
                target[kind, x, side] = out
            else:
                target[kind, side, x] = out


def chunk_kernel(step, count, part_ref, pick_ref, place_ref, scale_ref, *refs):
    sources, refs = refs[:count], refs[-17 - count :]
    outs, saved = refs[:2], refs[2:7]
    kept, buffers = refs[7:12], refs[12 : 12 + count]
    homes, sems = refs[-5:-3], refs[-3:]
    keep_ref, send_ref = homes
    rows_ref, cot_ref, hidden_ref, d_gate_ref, d_up_ref = kept
    pieces, (w_gate, w_up, w_down) = buffers[:-3], buffers[-3:]
    rows, capacity = rows_ref.shape[0], pick_ref.shape[2]
    def piece_loads(kind):
        copies = []
        for i, (source, target) in enumerate(zip(sources[:-3], pieces)):
            if len(source.shape) == 3:
                source, target = source.at[kind], target.at[kind]
            elif i % 5 != 3 + kind:
                continue
            copies.append(pltpu.make_async_copy(source, target, sems[0].at[kind, i]))
        return copies

    weight_loads = [
        pltpu.make_async_copy(source, target, sems[0].at[0, count - 3 + i])
        for i, (source, target) in enumerate(zip(sources[-3:], buffers[-3:]))
    ]
    stores = [
        pltpu.make_async_copy(source, target.at[pl.ds(step * rows, rows)], sems[1].at[i])
        for i, (source, target) in enumerate(zip(kept, saved))
    ]
    sends = [
        pltpu.make_async_copy(source.at[kind], target.at[kind], sems[2].at[kind, i])
        for kind in range(2)
        for i, (source, target) in enumerate(zip(homes, outs))
    ]
    token_loads, cot_loads = piece_loads(0), piece_loads(1)
    for copy in [*token_loads, *weight_loads[:2], weight_loads[2], *cot_loads]:
        copy.start()

    def store_rows(group, found):
        rows_ref[pl.ds(group * capacity, capacity), :] = found.astype(jnp.bfloat16)

    def store_cot(group, found):
        span = pl.ds(group * capacity, capacity)
        cot_ref[span, :] = (found * scale_ref[span, :]).astype(jnp.bfloat16)

    part = part_ref[0]
    width = w_down.shape[1] // 2
    halves = [slice(half * width, (half + 1) * width) for half in range(2)]
    for copy in token_loads:
        copy.wait()
    take_rows(0, pick_ref, pieces, store_rows)
    stores[0].start()
    expert_in = rows_ref[...]
    weight_loads[0].wait()
    gate_val = mxu(expert_in, w_gate[...])
    weight_loads[1].wait()
    up_val = mxu(expert_in, w_up[...])
    act_val, act_slope = silu_parts(gate_val)
    hidden = (act_val * up_val).astype(jnp.bfloat16)
    hidden_ref[...] = hidden
    stores[2].start()
    weight_loads[2].wait()
    for half, span in enumerate(halves):
        out = (mxu(hidden, w_down[:, span]) * scale_ref[...]).astype(jnp.bfloat16)
        spread_rows(0, part, half, out, place_ref, keep_ref, send_ref)
    for send in sends[:2]:
        send.start()
    for copy in cot_loads:
        copy.wait()
    take_rows(1, pick_ref, pieces, store_cot)
    stores[1].start()
    d_hidden = mxu(cot_ref[...], w_down[...], ((1,), (1,)))
    d_gate = (d_hidden * up_val * act_slope).astype(jnp.bfloat16)
    d_up = (d_hidden * act_val).astype(jnp.bfloat16)
    d_gate_ref[...] = d_gate
    d_up_ref[...] = d_up
    stores[3].start()
    stores[4].start()
    for half, span in enumerate(halves):
        grad = mxu(d_gate, w_gate[span, :], ((1,), (1,))) + mxu(d_up, w_up[span, :], ((1,), (1,)))
        spread_rows(1, part, half, grad.astype(jnp.bfloat16), place_ref, keep_ref, send_ref)
    for send in sends[2:]:
        send.start()
    for copy in stores + sends:
        copy.wait()


def run_chunk(step, tables, sources, saved_shapes, saved, marks):
    def array(a):
        return jax.ShapeDtypeStruct(a.shape, a.dtype)

    def scratch(a):
        return pltpu.VMEM(a.shape, a.dtype)

    kinds, half_rows, model_width = sources[0].shape
    home = jax.ShapeDtypeStruct((kinds, 2, 2, 2 * half_rows, model_width // 2), jnp.bfloat16)
    vmem, hbm = pl.BlockSpec(memory_space=pltpu.VMEM), pl.BlockSpec(memory_space=pl.ANY)
    rows = tables[-1].shape[0]
    first_saved = len(tables) + len(sources)
    return call_kernel(
        functools.partial(chunk_kernel, step, len(sources)),
        "chunk",
        [home, home, *saved_shapes],
        [*tables, *sources, *saved, *marks],
        vmem=60 * 2**20,
        flops=12 * rows * sources[-1].shape[0] * sources[-1].shape[1],
        in_specs=[pl.BlockSpec(memory_space=pltpu.SMEM)]
        + [vmem] * (len(tables) - 1)
        + [hbm] * (len(sources) + len(saved))
        + [vmem] * len(marks),
        out_specs=[hbm] * (2 + len(saved_shapes)),
        input_output_aliases={first_saved + i: 2 + i for i in range(len(saved))},
        scratch_shapes=[pltpu.VMEM((rows, s.shape[1]), s.dtype) for s in saved_shapes]
        + [scratch(source) for source in sources]
        + [scratch(home)] * 2
        + [pltpu.SemaphoreType.DMA(n) for n in ((2, len(sources)), (len(saved_shapes),), (2, 2))],
    )


def dense_plan(tokens, routes, kept_mask, gate_probs, output_grad, w_gate, w_up, w_down):
    dp_size = lax.axis_size("dp")
    line = dp_size // 4
    tok_rows, top_count = routes.shape
    capacity = tok_rows * top_count // dp_size
    model_width = tokens.shape[1]
    hidden_part = w_gate.shape[2]
    rows = 4 * capacity
    part = lax.axis_index("expert")
    w_gate, w_up, w_down = w_gate[0], w_up[0], w_down[0]

    table = jnp.concatenate(
        [routes.T.astype(jnp.float32), kept_mask.T.astype(jnp.float32), gate_probs.T], axis=0
    )
    part_arg = part.astype(jnp.int32).reshape(1)
    mine, other, table = own_halves(part_arg, tokens, output_grad, table)
    table = gather_small(table, line)
    chosen, kept, probs = jnp.split(table, 3, axis=3)
    expert = lax.axis_index("dp").astype(jnp.float32)
    hit = jnp.where(chosen == expert, kept, 0.0)
    used = jnp.sum(hit, axis=3)
    weight = jnp.sum(hit * probs, axis=3)
    kept_count = jnp.sum(used)
    earlier = jnp.triu(jnp.ones((tok_rows, tok_rows), jnp.bfloat16), 1)
    rank = jnp.einsum(
        "sabt,tu->sabu", used.astype(jnp.bfloat16), earlier, preferred_element_type=jnp.float32
    )
    slots = jnp.arange(capacity, dtype=jnp.float32)[:, None]
    pick = jnp.where(rank[..., None, :] == slots, used[..., None, :], 0.0)
    row_weight = jnp.sum(pick * weight[..., None, :], axis=4).reshape(line, rows, 1)
    pick = pick.astype(jnp.bfloat16)
    place = jnp.swapaxes(pick, 3, 4)
    pick_in = jnp.where(part == 0, pick, jnp.roll(pick, tok_rows // 2, axis=4))

    pieces, gathered = gather_line(mine, other, line)

    def saved_array(width):
        return jax.ShapeDtypeStruct((line * rows, width), jnp.bfloat16)

    saved_shapes = [saved_array(model_width)] * 2 + [saved_array(hidden_part)] * 3
    saved, returns = [], []

    def back(steps, *stages):
        return [returns[-steps][1][i] for i in stages] if steps <= len(returns) else []

    for step in range(line):
        keep, send, *saved = run_chunk(
            step,
            [part_arg, pick_in[step], place[step], row_weight[step]],
            [*pieces[step], w_gate, w_up, w_down],
            saved_shapes,
            saved,
            [],
        )
        before = ([], [], [])
        if step == line - 1:
            before = ([], back(2, 2), back(1, 2) + [returns[-2][0]])
        returns.append(send_home(keep, send, step, before))
    expert_in, cot_rows, hidden, d_gate, d_up = saved
    inv_count = 1.0 / jnp.maximum(kept_count, 1.0)
    by_row = ((0,), (0,))
    grad_down = (mxu(hidden, cot_rows, by_row) * inv_count).astype(jnp.bfloat16)
    grad_gate = (mxu(expert_in, d_gate, by_row) * inv_count).astype(jnp.bfloat16)
    grad_up = (mxu(expert_in, d_up, by_row) * inv_count).astype(jnp.bfloat16)
    results = sum(total.astype(jnp.float32) for total, _ in returns).astype(jnp.bfloat16)
    return (results[0], results[1], grad_gate[None], grad_up[None], grad_down[None])


def per_device(tokens, routes, kept_mask, gate_probs, output_grad, w_gate, w_up, w_down):
    dp_size = lax.axis_size("dp")
    local_experts = w_gate.shape[0]
    top_count = routes.shape[1]
    dense = (
        local_experts == 1
        and lax.axis_size("expert") == 2
        and dp_size % 4 == 0
        and 2 * top_count >= dp_size
    )
    plan = dense_plan if dense else routed_plan
    return plan(tokens, routes, kept_mask, gate_probs, output_grad, w_gate, w_up, w_down)


def solution(mesh):
    placed = (
        P("dp", None),
        P("dp", None),
        P("dp", None),
        P("dp", None),
        P("dp", None),
        P("dp", None, "expert"),
        P("dp", None, "expert"),
        P("dp", "expert", None),
    )
    return jax.shard_map(
        per_device,
        mesh=mesh,
        in_specs=placed,
        out_specs=(
            P("dp", "expert"),
            P("dp", "expert"),
            P("dp", None, "expert"),
            P("dp", None, "expert"),
            P("dp", "expert", None),
        ),
        check_vma=False,
    )
```

```python
import functools
import math

import jax
import jax.numpy as jnp
from jax import lax
from jax.experimental import pallas as pl
from jax.experimental.pallas import tpu as pltpu
from jax.sharding import PartitionSpec as P


def silu_parts(gate_val):
    sigmoid_val = jax.nn.sigmoid(gate_val)
    return (gate_val * sigmoid_val, sigmoid_val * (1.0 + gate_val * (1.0 - sigmoid_val)))


def slot_layout(routes, experts):
    tok_rows, top_count = routes.shape
    pair_count = tok_rows * top_count
    flat_routes = routes.reshape(pair_count)
    onehot = (flat_routes[:, None] == jnp.arange(experts, dtype=jnp.int32)[None, :]).astype(
        jnp.int32
    )
    before = jnp.cumsum(onehot, axis=0) - onehot
    slot_index = jnp.sum(before * onehot, axis=1)
    capacity = pair_count // experts
    dest_index = flat_routes * capacity + slot_index
    source = (
        jnp.zeros((pair_count,), jnp.int32)
        .at[dest_index]
        .set(jnp.arange(pair_count, dtype=jnp.int32))
    )
    return (dest_index, source, onehot)


def to_experts(rows_in, dp_size, local_experts):
    capacity = rows_in.shape[1]
    width = rows_in.shape[2]
    grouped = rows_in.reshape(dp_size, local_experts, capacity, width)
    return jnp.swapaxes(grouped, 0, 1).reshape(local_experts, dp_size * capacity, width)


def from_experts(values, dp_size):
    local_experts, slot_total, width = values.shape
    capacity = slot_total // dp_size
    grouped = values.reshape(local_experts, dp_size, capacity, width)
    return jnp.swapaxes(grouped, 0, 1).reshape(dp_size * local_experts, capacity, width)


def combine(back_rows, dest_index, factor, tok_rows, top_count):
    width = back_rows.shape[2]
    picked = back_rows.reshape(-1, width)[dest_index].astype(jnp.float32) * factor[:, None]
    return jnp.sum(picked.reshape(tok_rows, top_count, width), axis=1)


def routed_plan(tokens, routes, kept_mask, gate_probs, output_grad, w_gate, w_up, w_down):
    dp_size = lax.axis_size("dp")
    part_count = lax.axis_size("expert")
    local_experts, model_width, hidden_part = w_gate.shape
    experts = local_experts * dp_size
    tok_rows, top_count = routes.shape
    capacity = tok_rows * top_count // experts
    col_width = model_width // part_count
    dest_index, source, onehot = slot_layout(routes, experts)
    keep_float = kept_mask.reshape(-1).astype(jnp.float32)
    weight_flat = keep_float * gate_probs.reshape(-1)
    src_token = source // top_count
    src_keep = keep_float[source]
    src_weight = weight_flat[source]
    col_start = lax.axis_index("expert") * col_width
    token_src = lax.dynamic_slice_in_dim(tokens, col_start, col_width, 1)
    cot_src = lax.dynamic_slice_in_dim(output_grad, col_start, col_width, 1)
    send_width = token_src.shape[1]
    rows_send = (token_src[src_token].astype(jnp.float32) * src_keep[:, None]).astype(jnp.bfloat16)
    rows_send = rows_send.reshape(experts, capacity, send_width)
    cot_send = (cot_src[src_token].astype(jnp.float32) * src_weight[:, None]).astype(jnp.bfloat16)
    cot_send = cot_send.reshape(experts, capacity, send_width)
    totals = jnp.sum(onehot.astype(jnp.float32) * keep_float[:, None], axis=0)
    totals = lax.psum(totals, "dp")
    kept_count = lax.dynamic_slice_in_dim(
        totals, lax.axis_index("dp") * local_experts, local_experts
    )
    rows_in = lax.all_to_all(rows_send, "dp", split_axis=0, concat_axis=0, tiled=True)
    cot_in = lax.all_to_all(cot_send, "dp", split_axis=0, concat_axis=0, tiled=True)
    rows_in = lax.all_gather(rows_in, "expert", axis=2, tiled=True)
    cot_in = lax.all_gather(cot_in, "expert", axis=2, tiled=True)
    expert_in = to_experts(rows_in, dp_size, local_experts)
    cot_full = to_experts(cot_in, dp_size, local_experts)
    down_cols = lax.all_to_all(w_down, "expert", split_axis=2, concat_axis=1, tiled=True)
    gate_rows, up_rows = (
        lax.all_to_all(w_gate, "expert", split_axis=1, concat_axis=2, tiled=True),
        lax.all_to_all(w_up, "expert", split_axis=1, concat_axis=2, tiled=True),
    )
    gate_val = jnp.einsum("lsd,ldh->lsh", expert_in, w_gate, preferred_element_type=jnp.float32)
    up_val = jnp.einsum("lsd,ldh->lsh", expert_in, w_up, preferred_element_type=jnp.float32)
    act_val, act_slope = silu_parts(gate_val)
    hidden = (act_val * up_val).astype(jnp.bfloat16)
    expert_out = jnp.einsum(
        "lsh,lhc->lsc",
        lax.all_gather(hidden, "expert", axis=2, tiled=True),
        down_cols,
        preferred_element_type=jnp.float32,
    ).astype(jnp.bfloat16)
    out_back = lax.all_to_all(
        from_experts(expert_out, dp_size), "dp", split_axis=0, concat_axis=0, tiled=True
    )
    output = combine(out_back, dest_index, weight_flat, tok_rows, top_count).astype(jnp.bfloat16)
    d_hidden = jnp.einsum("lsd,lhd->lsh", cot_full, w_down, preferred_element_type=jnp.float32)
    d_gate = (d_hidden * up_val * act_slope).astype(jnp.bfloat16)
    d_up = (d_hidden * act_val).astype(jnp.bfloat16)
    inv_count = (1.0 / jnp.maximum(kept_count, 1.0))[:, None, None]
    grad_down = (
        jnp.einsum("lsh,lsd->lhd", hidden, cot_full, preferred_element_type=jnp.float32) * inv_count
    ).astype(jnp.bfloat16)
    grad_gate = (
        jnp.einsum("lsd,lsh->ldh", expert_in, d_gate, preferred_element_type=jnp.float32)
        * inv_count
    ).astype(jnp.bfloat16)
    grad_up = (
        jnp.einsum("lsd,lsh->ldh", expert_in, d_up, preferred_element_type=jnp.float32) * inv_count
    ).astype(jnp.bfloat16)
    running = jnp.einsum(
        "lsh,lch->lsc",
        lax.all_gather(d_gate, "expert", axis=2, tiled=True),
        gate_rows,
        preferred_element_type=jnp.float32,
    )
    d_rows = (
        running
        + jnp.einsum(
            "lsh,lch->lsc",
            lax.all_gather(d_up, "expert", axis=2, tiled=True),
            up_rows,
            preferred_element_type=jnp.float32,
        )
    ).astype(jnp.bfloat16)
    grad_back = lax.all_to_all(
        from_experts(d_rows, dp_size), "dp", split_axis=0, concat_axis=0, tiled=True
    )
    input_grad = combine(grad_back, dest_index, keep_float, tok_rows, top_count).astype(
        jnp.bfloat16
    )
    return (output, input_grad, grad_gate, grad_up, grad_down)


def swap(values, axis_name, bit):
    size = lax.axis_size(axis_name)
    return lax.ppermute(values, axis_name, [(i, i ^ bit) for i in range(size)])


def shift(values, steps):
    size = lax.axis_size("dp")
    return lax.ppermute(values, "dp", [(i, (i + 4 * steps) % size) for i in range(size)])


def cut_halves(part_ref, tokens, cots, table, mine, other, table_out):
    table_out[...] = table[...]
    rows = tokens.shape[0] // 2
    own = pl.multiple_of(part_ref[0] * rows, rows)
    rest = pl.multiple_of(rows - part_ref[0] * rows, rows)
    for kind, values in enumerate((tokens, cots)):
        mine[kind] = values[pl.ds(own, rows), :]
        other[kind] = values[pl.ds(rest, rows), :]


def own_halves(part_arg, tokens, cots, table):
    shape = jax.ShapeDtypeStruct((2, tokens.shape[0] // 2, tokens.shape[1]), tokens.dtype)
    vmem = pl.BlockSpec(memory_space=pltpu.VMEM)
    return call_kernel(
        cut_halves,
        "own_halves",
        [shape, shape, jax.ShapeDtypeStruct(table.shape, table.dtype)],
        [part_arg, tokens, cots, table],
        in_specs=[pl.BlockSpec(memory_space=pltpu.SMEM), vmem, vmem, vmem],
    )


def cut_kinds(rest, across, *refs):
    rest_out, across_out, mark, sems = refs[-4:]
    mark[...] = jnp.zeros_like(mark)
    copies = [
        pltpu.make_async_copy(rest.at[0], rest_out, sems.at[0]),
        pltpu.make_async_copy(across.at[1], across_out, sems.at[1]),
    ]
    for copy in copies:
        copy.start()
    for copy in copies:
        copy.wait()


def kinds_apart(rest, across, after):
    hbm = pl.BlockSpec(memory_space=pl.ANY)
    shape = jax.ShapeDtypeStruct(rest.shape[1:], rest.dtype)
    return call_kernel(
        cut_kinds,
        "cut_kinds",
        [shape, shape, jax.ShapeDtypeStruct((8, 128), jnp.float32)],
        [rest, across, *after],
        in_specs=[hbm] * (2 + len(after)),
        scratch_shapes=[pltpu.SemaphoreType.DMA((2,))],
    )


def gather_line(mine, other, line, run_first):
    halves = [mine]
    for _ in range(line - 1):
        halves.append(shift(halves[-1], 1))
    steps = []
    for step, half in enumerate(halves):
        rest = swap(half, "expert", 1) if step else other
        across = swap(half, "dp", 2)
        if step:
            after = [run_first(steps[0])] if step == line - 1 else []
            tokens, cots, _ = kinds_apart(rest, across, after)
            last = (swap(tokens, "dp", 2), swap(cots, "expert", 1))
        else:
            last = (swap(across, "expert", 1),)
        pieces = (half, rest, across) + last
        steps.append(pieces + tuple(swap(piece, "dp", 1) for piece in pieces))
    return steps


def gather_small(values, line):
    lines = jnp.stack([values] + [shift(values, step) for step in range(1, line)])
    pairs = jnp.stack([lines, swap(lines, "dp", 2)], axis=1)
    return jnp.stack([pairs, swap(pairs, "dp", 1)], axis=2)


def mxu(a, b, dims=((1,), (0,))):
    return lax.dot_general(a, b, (dims, ((), ())), preferred_element_type=jnp.float32)


def add_to(target, *terms):
    target[...] = sum(term.astype(jnp.float32) for term in terms).astype(jnp.bfloat16)


def add_cores(keep, got, *refs):
    away_out, away_grad, home, mark = refs[-4:]
    mark[...] = jnp.zeros_like(mark)
    add_to(away_out, keep[0, 1], got[0, 1])
    add_to(away_grad, keep[1, 1], got[1, 1])
    add_to(home, keep[:, 0], got[:, 0])


def add_first(home, away_out, away_grad, *refs):
    last_out, last_grad, mark = refs[-3:]
    mark[...] = jnp.zeros_like(mark)
    add_to(last_out, home[0, 1], away_out[1])
    add_to(last_grad, home[1, 1], away_grad[1])


def add_last(extra_count, home, away_out, away_grad, last_out, last_grad, *refs):
    total, mark = refs[-2:]
    extra = refs[:extra_count]
    mark[...] = jnp.zeros_like(mark)
    add_to(total.at[0], home[0, 0], away_out[0], last_out[...], *[e[0] for e in extra])
    add_to(total.at[1], home[1, 0], away_grad[0], last_grad[...], *[e[1] for e in extra])


def call_kernel(kernel, name, shapes, args, flops=0, vmem=8 * 2**20, **options):
    space = pl.BlockSpec(memory_space=pltpu.VMEM)
    moved = sum(math.prod(a.shape) * a.dtype.itemsize for a in [*args, *shapes])
    return pl.pallas_call(
        kernel,
        out_shape=shapes,
        in_specs=options.pop("in_specs", [space] * len(args)),
        out_specs=options.pop("out_specs", [space] * len(shapes)),
        compiler_params=pltpu.CompilerParams(vmem_limit_bytes=vmem),
        cost_estimate=pl.CostEstimate(flops=flops, bytes_accessed=moved, transcendentals=0),
        name=name,
        **options,
    )(*args)


def send_home(keep, send, extra, before):
    def array(*shape):
        return jax.ShapeDtypeStruct(shape, jnp.bfloat16)

    rows, columns = keep.shape[3:]
    pair, single = array(2, rows, columns), array(rows, columns)
    mark = jax.ShapeDtypeStruct((8, 128), jnp.float32)
    got = swap(send, "dp", 1)
    away_out, away_grad, home, mark_cores = call_kernel(
        add_cores, "add_cores", [pair, pair, array(2, 2, rows, columns), mark], [keep, got]
    )
    away = (swap(away_out, "dp", 2), swap(away_grad, "expert", 1))
    *lasts, mark_first = call_kernel(add_first, "add_first", [single, single, mark], [home, *away, *before])
    last = (swap(lasts[0], "expert", 1), swap(lasts[1], "dp", 2))
    total, mark_last = call_kernel(
        functools.partial(add_last, len(extra)),
        "add_last",
        [pair, mark],
        [home, *away, *last, *extra],
    )
    return total, mark_last


def take_rows(kind, pick_ref, pieces, store):
    for x in range(2):
        for core in range(2):
            half, rest, across, *last = pieces[core * len(pieces) // 2 : (core + 1) * len(pieces) // 2]
            if x == 0:
                block = jnp.concatenate([half[kind], rest[kind]], axis=0)
            else:
                rows = last[kind][...] if len(last) == 2 else last[0][kind]
                block = jnp.concatenate([across[kind], rows], axis=0)
            store(2 * x + core, mxu(pick_ref[x, core], block))


def spread_rows(kind, part, half, rows, place_ref, keep_ref, send_ref):
    capacity = rows.shape[0] // 4
    side = half ^ part
    for x in range(2):
        for core in range(2):
            group = 2 * x + core
            piece = rows[group * capacity : (group + 1) * capacity]
            out = mxu(place_ref[x, core], piece).astype(jnp.bfloat16)
            target = keep_ref if core == 0 else send_ref
            if kind == 0:
                target[kind, x, side] = out
            else:
                target[kind, side, x] = out


def chunk_kernel(step, count, part_ref, pick_ref, place_ref, scale_ref, *refs):
    sources, refs = refs[:count], refs[-17 - count :]
    outs, saved = refs[:2], refs[2:7]
    kept, buffers = refs[7:12], refs[12 : 12 + count]
    homes, sems = refs[-5:-3], refs[-3:]
    keep_ref, send_ref = homes
    rows_ref, cot_ref, hidden_ref, d_gate_ref, d_up_ref = kept
    pieces, (w_gate, w_up, w_down) = buffers[:-3], buffers[-3:]
    rows, capacity = rows_ref.shape[0], pick_ref.shape[2]
    def piece_loads(kind):
        copies = []
        for i, (source, target) in enumerate(zip(sources[:-3], pieces)):
            if len(source.shape) == 3:
                source, target = source.at[kind], target.at[kind]
            elif i % 5 != 3 + kind:
                continue
            copies.append(pltpu.make_async_copy(source, target, sems[0].at[kind, i]))
        return copies

    weight_loads = [
        pltpu.make_async_copy(source, target, sems[0].at[0, count - 3 + i])
        for i, (source, target) in enumerate(zip(sources[-3:], buffers[-3:]))
    ]
    stores = [
        pltpu.make_async_copy(source, target.at[pl.ds(step * rows, rows)], sems[1].at[i])
        for i, (source, target) in enumerate(zip(kept, saved))
    ]
    sends = [
        pltpu.make_async_copy(source.at[kind], target.at[kind], sems[2].at[kind, i])
        for kind in range(2)
        for i, (source, target) in enumerate(zip(homes, outs))
    ]
    token_loads, cot_loads = piece_loads(0), piece_loads(1)
    for copy in [*token_loads, *weight_loads[:2], weight_loads[2], *cot_loads]:
        copy.start()

    def store_rows(group, found):
        rows_ref[pl.ds(group * capacity, capacity), :] = found.astype(jnp.bfloat16)

    def store_cot(group, found):
        span = pl.ds(group * capacity, capacity)
        cot_ref[span, :] = (found * scale_ref[span, :]).astype(jnp.bfloat16)

    part = part_ref[0]
    width = w_down.shape[1] // 2
    halves = [slice(half * width, (half + 1) * width) for half in range(2)]
    for copy in token_loads:
        copy.wait()
    take_rows(0, pick_ref, pieces, store_rows)
    stores[0].start()
    expert_in = rows_ref[...]
    weight_loads[0].wait()
    gate_val = mxu(expert_in, w_gate[...])
    weight_loads[1].wait()
    up_val = mxu(expert_in, w_up[...])
    act_val, act_slope = silu_parts(gate_val)
    hidden = (act_val * up_val).astype(jnp.bfloat16)
    hidden_ref[...] = hidden
    stores[2].start()
    weight_loads[2].wait()
    for half, span in enumerate(halves):
        out = (mxu(hidden, w_down[:, span]) * scale_ref[...]).astype(jnp.bfloat16)
        spread_rows(0, part, half, out, place_ref, keep_ref, send_ref)
    for send in sends[:2]:
        send.start()
    for copy in cot_loads:
        copy.wait()
    take_rows(1, pick_ref, pieces, store_cot)
    stores[1].start()
    d_hidden = mxu(cot_ref[...], w_down[...], ((1,), (1,)))
    d_gate = (d_hidden * up_val * act_slope).astype(jnp.bfloat16)
    d_up = (d_hidden * act_val).astype(jnp.bfloat16)
    d_gate_ref[...] = d_gate
    d_up_ref[...] = d_up
    stores[3].start()
    stores[4].start()
    for half, span in enumerate(halves):
        grad = mxu(d_gate, w_gate[span, :], ((1,), (1,))) + mxu(d_up, w_up[span, :], ((1,), (1,)))
        spread_rows(1, part, half, grad.astype(jnp.bfloat16), place_ref, keep_ref, send_ref)
    for send in sends[2:]:
        send.start()
    for copy in stores + sends:
        copy.wait()


def run_chunk(step, tables, sources, saved_shapes, saved, marks):
    def array(a):
        return jax.ShapeDtypeStruct(a.shape, a.dtype)

    def scratch(a):
        return pltpu.VMEM(a.shape, a.dtype)

    kinds, half_rows, model_width = sources[0].shape
    home = jax.ShapeDtypeStruct((kinds, 2, 2, 2 * half_rows, model_width // 2), jnp.bfloat16)
    vmem, hbm = pl.BlockSpec(memory_space=pltpu.VMEM), pl.BlockSpec(memory_space=pl.ANY)
    rows = tables[-1].shape[0]
    first_saved = len(tables) + len(sources)
    return call_kernel(
        functools.partial(chunk_kernel, step, len(sources)),
        "chunk",
        [home, home, *saved_shapes],
        [*tables, *sources, *saved, *marks],
        vmem=60 * 2**20,
        flops=12 * rows * sources[-1].shape[0] * sources[-1].shape[1],
        in_specs=[pl.BlockSpec(memory_space=pltpu.SMEM)]
        + [vmem] * (len(tables) - 1)
        + [hbm] * (len(sources) + len(saved))
        + [vmem] * len(marks),
        out_specs=[hbm] * (2 + len(saved_shapes)),
        input_output_aliases={first_saved + i: 2 + i for i in range(len(saved))},
        scratch_shapes=[pltpu.VMEM((rows, s.shape[1]), s.dtype) for s in saved_shapes]
        + [scratch(source) for source in sources]
        + [scratch(home)] * 2
        + [pltpu.SemaphoreType.DMA(n) for n in ((2, len(sources)), (len(saved_shapes),), (2, 2))],
    )


def dense_plan(tokens, routes, kept_mask, gate_probs, output_grad, w_gate, w_up, w_down):
    dp_size = lax.axis_size("dp")
    line = dp_size // 4
    tok_rows, top_count = routes.shape
    capacity = tok_rows * top_count // dp_size
    model_width = tokens.shape[1]
    hidden_part = w_gate.shape[2]
    rows = 4 * capacity
    part = lax.axis_index("expert")
    w_gate, w_up, w_down = w_gate[0], w_up[0], w_down[0]

    table = jnp.concatenate(
        [routes.T.astype(jnp.float32), kept_mask.T.astype(jnp.float32), gate_probs.T], axis=0
    )
    part_arg = part.astype(jnp.int32).reshape(1)
    mine, other, table = own_halves(part_arg, tokens, output_grad, table)
    table = gather_small(table, line)
    chosen, kept, probs = jnp.split(table, 3, axis=3)
    expert = lax.axis_index("dp").astype(jnp.float32)
    hit = jnp.where(chosen == expert, kept, 0.0)
    used = jnp.sum(hit, axis=3)
    weight = jnp.sum(hit * probs, axis=3)
    kept_count = jnp.sum(used)
    earlier = jnp.triu(jnp.ones((tok_rows, tok_rows), jnp.bfloat16), 1)
    rank = jnp.einsum(
        "sabt,tu->sabu", used.astype(jnp.bfloat16), earlier, preferred_element_type=jnp.float32
    )
    slots = jnp.arange(capacity, dtype=jnp.float32)[:, None]
    pick = jnp.where(rank[..., None, :] == slots, used[..., None, :], 0.0)
    row_weight = jnp.sum(pick * weight[..., None, :], axis=4).reshape(line, rows, 1)
    pick = pick.astype(jnp.bfloat16)
    place = jnp.swapaxes(pick, 3, 4)
    pick_in = jnp.where(part == 0, pick, jnp.roll(pick, tok_rows // 2, axis=4))


    def saved_array(width):
        return jax.ShapeDtypeStruct((line * rows, width), jnp.bfloat16)

    saved_shapes = [saved_array(model_width)] * 2 + [saved_array(hidden_part)] * 3
    done = []

    def chunk(step, rows_in):
        saved = done[-1][2:] if done else []
        done.append(
            run_chunk(
                step,
                [part_arg, pick_in[step], place[step], row_weight[step]],
                [*rows_in, w_gate, w_up, w_down],
                saved_shapes,
                saved,
                [],
            )
        )
        return done[-1][1]

    pieces = gather_line(mine, other, line, functools.partial(chunk, 0))
    for step in range(1, line):
        chunk(step, pieces[step])
    saved = done[-1][2:]

    down, up, before = [], [], []
    for step in range(line // 2, 0, -1):
        total, mark = send_home(*done[step][:2], down, [])
        before = before or [mark]
        down = [shift(total, -1)]
    for step in range(line // 2 + 1, line):
        up = [shift(send_home(*done[step][:2], up, before)[0], 1)]
    returns = [send_home(*done[0][:2], [], [])[0], *down, *up]
    expert_in, cot_rows, hidden, d_gate, d_up = saved
    inv_count = 1.0 / jnp.maximum(kept_count, 1.0)
    by_row = ((0,), (0,))
    grad_down = (mxu(hidden, cot_rows, by_row) * inv_count).astype(jnp.bfloat16)
    grad_gate = (mxu(expert_in, d_gate, by_row) * inv_count).astype(jnp.bfloat16)
    grad_up = (mxu(expert_in, d_up, by_row) * inv_count).astype(jnp.bfloat16)
    results = sum(total.astype(jnp.float32) for total in returns).astype(jnp.bfloat16)
    return (results[0], results[1], grad_gate[None], grad_up[None], grad_down[None])


def per_device(tokens, routes, kept_mask, gate_probs, output_grad, w_gate, w_up, w_down):
    dp_size = lax.axis_size("dp")
    local_experts = w_gate.shape[0]
    top_count = routes.shape[1]
    dense = (
        local_experts == 1
        and lax.axis_size("expert") == 2
        and dp_size % 4 == 0
        and 2 * top_count >= dp_size
    )
    plan = dense_plan if dense else routed_plan
    return plan(tokens, routes, kept_mask, gate_probs, output_grad, w_gate, w_up, w_down)


def solution(mesh):
    placed = (
        P("dp", None),
        P("dp", None),
        P("dp", None),
        P("dp", None),
        P("dp", None),
        P("dp", None, "expert"),
        P("dp", None, "expert"),
        P("dp", "expert", None),
    )
    return jax.shard_map(
        per_device,
        mesh=mesh,
        in_specs=placed,
        out_specs=(
            P("dp", "expert"),
            P("dp", "expert"),
            P("dp", None, "expert"),
            P("dp", None, "expert"),
            P("dp", "expert", None),
        ),
        check_vma=False,
    )
```

```python
import functools
import math

import jax
import jax.numpy as jnp
from jax import lax
from jax.experimental import pallas as pl
from jax.experimental.pallas import tpu as pltpu
from jax.sharding import PartitionSpec as P


def silu_parts(gate_val):
    sigmoid_val = jax.nn.sigmoid(gate_val)
    return (gate_val * sigmoid_val, sigmoid_val * (1.0 + gate_val * (1.0 - sigmoid_val)))


def slot_layout(routes, experts):
    tok_rows, top_count = routes.shape
    pair_count = tok_rows * top_count
    flat_routes = routes.reshape(pair_count)
    onehot = (flat_routes[:, None] == jnp.arange(experts, dtype=jnp.int32)[None, :]).astype(
        jnp.int32
    )
    before = jnp.cumsum(onehot, axis=0) - onehot
    slot_index = jnp.sum(before * onehot, axis=1)
    capacity = pair_count // experts
    dest_index = flat_routes * capacity + slot_index
    source = (
        jnp.zeros((pair_count,), jnp.int32)
        .at[dest_index]
        .set(jnp.arange(pair_count, dtype=jnp.int32))
    )
    return (dest_index, source, onehot)


def to_experts(rows_in, dp_size, local_experts):
    capacity = rows_in.shape[1]
    width = rows_in.shape[2]
    grouped = rows_in.reshape(dp_size, local_experts, capacity, width)
    return jnp.swapaxes(grouped, 0, 1).reshape(local_experts, dp_size * capacity, width)


def from_experts(values, dp_size):
    local_experts, slot_total, width = values.shape
    capacity = slot_total // dp_size
    grouped = values.reshape(local_experts, dp_size, capacity, width)
    return jnp.swapaxes(grouped, 0, 1).reshape(dp_size * local_experts, capacity, width)


def combine(back_rows, dest_index, factor, tok_rows, top_count):
    width = back_rows.shape[2]
    picked = back_rows.reshape(-1, width)[dest_index].astype(jnp.float32) * factor[:, None]
    return jnp.sum(picked.reshape(tok_rows, top_count, width), axis=1)


def routed_plan(tokens, routes, kept_mask, gate_probs, output_grad, w_gate, w_up, w_down):
    dp_size = lax.axis_size("dp")
    part_count = lax.axis_size("expert")
    local_experts, model_width, hidden_part = w_gate.shape
    experts = local_experts * dp_size
    tok_rows, top_count = routes.shape
    capacity = tok_rows * top_count // experts
    col_width = model_width // part_count
    dest_index, source, onehot = slot_layout(routes, experts)
    keep_float = kept_mask.reshape(-1).astype(jnp.float32)
    weight_flat = keep_float * gate_probs.reshape(-1)
    src_token = source // top_count
    src_keep = keep_float[source]
    src_weight = weight_flat[source]
    col_start = lax.axis_index("expert") * col_width
    token_src = lax.dynamic_slice_in_dim(tokens, col_start, col_width, 1)
    cot_src = lax.dynamic_slice_in_dim(output_grad, col_start, col_width, 1)
    send_width = token_src.shape[1]
    rows_send = (token_src[src_token].astype(jnp.float32) * src_keep[:, None]).astype(jnp.bfloat16)
    rows_send = rows_send.reshape(experts, capacity, send_width)
    cot_send = (cot_src[src_token].astype(jnp.float32) * src_weight[:, None]).astype(jnp.bfloat16)
    cot_send = cot_send.reshape(experts, capacity, send_width)
    totals = jnp.sum(onehot.astype(jnp.float32) * keep_float[:, None], axis=0)
    totals = lax.psum(totals, "dp")
    kept_count = lax.dynamic_slice_in_dim(
        totals, lax.axis_index("dp") * local_experts, local_experts
    )
    rows_in = lax.all_to_all(rows_send, "dp", split_axis=0, concat_axis=0, tiled=True)
    cot_in = lax.all_to_all(cot_send, "dp", split_axis=0, concat_axis=0, tiled=True)
    rows_in = lax.all_gather(rows_in, "expert", axis=2, tiled=True)
    cot_in = lax.all_gather(cot_in, "expert", axis=2, tiled=True)
    expert_in = to_experts(rows_in, dp_size, local_experts)
    cot_full = to_experts(cot_in, dp_size, local_experts)
    down_cols = lax.all_to_all(w_down, "expert", split_axis=2, concat_axis=1, tiled=True)
    gate_rows, up_rows = (
        lax.all_to_all(w_gate, "expert", split_axis=1, concat_axis=2, tiled=True),
        lax.all_to_all(w_up, "expert", split_axis=1, concat_axis=2, tiled=True),
    )
    gate_val = jnp.einsum("lsd,ldh->lsh", expert_in, w_gate, preferred_element_type=jnp.float32)
    up_val = jnp.einsum("lsd,ldh->lsh", expert_in, w_up, preferred_element_type=jnp.float32)
    act_val, act_slope = silu_parts(gate_val)
    hidden = (act_val * up_val).astype(jnp.bfloat16)
    expert_out = jnp.einsum(
        "lsh,lhc->lsc",
        lax.all_gather(hidden, "expert", axis=2, tiled=True),
        down_cols,
        preferred_element_type=jnp.float32,
    ).astype(jnp.bfloat16)
    out_back = lax.all_to_all(
        from_experts(expert_out, dp_size), "dp", split_axis=0, concat_axis=0, tiled=True
    )
    output = combine(out_back, dest_index, weight_flat, tok_rows, top_count).astype(jnp.bfloat16)
    d_hidden = jnp.einsum("lsd,lhd->lsh", cot_full, w_down, preferred_element_type=jnp.float32)
    d_gate = (d_hidden * up_val * act_slope).astype(jnp.bfloat16)
    d_up = (d_hidden * act_val).astype(jnp.bfloat16)
    inv_count = (1.0 / jnp.maximum(kept_count, 1.0))[:, None, None]
    grad_down = (
        jnp.einsum("lsh,lsd->lhd", hidden, cot_full, preferred_element_type=jnp.float32) * inv_count
    ).astype(jnp.bfloat16)
    grad_gate = (
        jnp.einsum("lsd,lsh->ldh", expert_in, d_gate, preferred_element_type=jnp.float32)
        * inv_count
    ).astype(jnp.bfloat16)
    grad_up = (
        jnp.einsum("lsd,lsh->ldh", expert_in, d_up, preferred_element_type=jnp.float32) * inv_count
    ).astype(jnp.bfloat16)
    running = jnp.einsum(
        "lsh,lch->lsc",
        lax.all_gather(d_gate, "expert", axis=2, tiled=True),
        gate_rows,
        preferred_element_type=jnp.float32,
    )
    d_rows = (
        running
        + jnp.einsum(
            "lsh,lch->lsc",
            lax.all_gather(d_up, "expert", axis=2, tiled=True),
            up_rows,
            preferred_element_type=jnp.float32,
        )
    ).astype(jnp.bfloat16)
    grad_back = lax.all_to_all(
        from_experts(d_rows, dp_size), "dp", split_axis=0, concat_axis=0, tiled=True
    )
    input_grad = combine(grad_back, dest_index, keep_float, tok_rows, top_count).astype(
        jnp.bfloat16
    )
    return (output, input_grad, grad_gate, grad_up, grad_down)


def swap(values, axis_name, bit):
    size = lax.axis_size(axis_name)
    return lax.ppermute(values, axis_name, [(i, i ^ bit) for i in range(size)])


def shift(values, steps):
    size = lax.axis_size("dp")
    return lax.ppermute(values, "dp", [(i, (i + 4 * steps) % size) for i in range(size)])


def cut_halves(part_ref, tokens, cots, table, mine, other, table_out, sems):
    rows = tokens.shape[0] // 2
    own = pl.multiple_of(part_ref[0] * rows, rows)
    rest = pl.multiple_of(rows - part_ref[0] * rows, rows)
    copies = []
    for kind, values in enumerate((tokens, cots)):
        for i, (start, out) in enumerate(((own, mine), (rest, other))):
            source = values.at[pl.ds(start, rows)]
            copies.append(pltpu.make_async_copy(source, out.at[kind], sems.at[kind, i]))
    for copy in copies:
        copy.start()
    table_out[...] = table[...]
    for copy in copies:
        copy.wait()


def own_halves(part_arg, tokens, cots, table):
    shape = jax.ShapeDtypeStruct((2, tokens.shape[0] // 2, tokens.shape[1]), tokens.dtype)
    vmem = pl.BlockSpec(memory_space=pltpu.VMEM)
    return call_kernel(
        cut_halves,
        "own_halves",
        [shape, shape, jax.ShapeDtypeStruct(table.shape, table.dtype)],
        [part_arg, tokens, cots, table],
        in_specs=[pl.BlockSpec(memory_space=pltpu.SMEM)] + [pl.BlockSpec(memory_space=pl.ANY)] * 2 + [vmem],
        scratch_shapes=[pltpu.SemaphoreType.DMA((2, 2))],
    )


def cut_kinds(rest, across, *refs):
    rest_out, across_out, mark, sems = refs[-4:]
    mark[...] = jnp.zeros_like(mark)
    copies = [
        pltpu.make_async_copy(rest.at[0], rest_out, sems.at[0]),
        pltpu.make_async_copy(across.at[1], across_out, sems.at[1]),
    ]
    for copy in copies:
        copy.start()
    for copy in copies:
        copy.wait()


def kinds_apart(rest, across, after):
    hbm = pl.BlockSpec(memory_space=pl.ANY)
    shape = jax.ShapeDtypeStruct(rest.shape[1:], rest.dtype)
    return call_kernel(
        cut_kinds,
        "cut_kinds",
        [shape, shape, jax.ShapeDtypeStruct((8, 128), jnp.float32)],
        [rest, across, *after],
        in_specs=[hbm] * (2 + len(after)),
        scratch_shapes=[pltpu.SemaphoreType.DMA((2,))],
    )


def gather_line(mine, other, line, run_first):
    halves = [mine]
    for _ in range(line - 1):
        halves.append(shift(halves[-1], 1))
    steps = []
    for step, half in enumerate(halves):
        rest = swap(half, "expert", 1) if step else other
        across = swap(half, "dp", 2)
        if step:
            after = [run_first(steps[0])] if step == line - 1 else []
            tokens, cots, _ = kinds_apart(rest, across, after)
            last = (swap(tokens, "dp", 2), swap(cots, "expert", 1))
        else:
            last = (swap(across, "expert", 1),)
        pieces = (half, rest, across) + last
        steps.append(pieces + tuple(swap(piece, "dp", 1) for piece in pieces))
    return steps


def gather_small(values, line):
    lines = jnp.stack([values] + [shift(values, step) for step in range(1, line)])
    pairs = jnp.stack([lines, swap(lines, "dp", 2)], axis=1)
    return jnp.stack([pairs, swap(pairs, "dp", 1)], axis=2)


def mxu(a, b, dims=((1,), (0,))):
    return lax.dot_general(a, b, (dims, ((), ())), preferred_element_type=jnp.float32)


def add_to(target, *terms):
    target[...] = sum(term.astype(jnp.float32) for term in terms).astype(jnp.bfloat16)


def add_cores(keep, got, *refs):
    away_out, away_grad, home, mark = refs[-4:]
    mark[...] = jnp.zeros_like(mark)
    add_to(away_out, keep[0, 1], got[0, 1])
    add_to(away_grad, keep[1, 1], got[1, 1])
    add_to(home, keep[:, 0], got[:, 0])


def add_first(home, away_out, away_grad, *refs):
    last_out, last_grad, mark = refs[-3:]
    mark[...] = jnp.zeros_like(mark)
    add_to(last_out, home[0, 1], away_out[1])
    add_to(last_grad, home[1, 1], away_grad[1])


def add_last(extra_count, home, away_out, away_grad, last_out, last_grad, *refs):
    total, mark = refs[-2:]
    extra = refs[:extra_count]
    mark[...] = jnp.zeros_like(mark)
    add_to(total.at[0], home[0, 0], away_out[0], last_out[...], *[e[0] for e in extra])
    add_to(total.at[1], home[1, 0], away_grad[0], last_grad[...], *[e[1] for e in extra])


def call_kernel(kernel, name, shapes, args, flops=0, vmem=8 * 2**20, **options):
    space = pl.BlockSpec(memory_space=pltpu.VMEM)
    moved = sum(math.prod(a.shape) * a.dtype.itemsize for a in [*args, *shapes])
    return pl.pallas_call(
        kernel,
        out_shape=shapes,
        in_specs=options.pop("in_specs", [space] * len(args)),
        out_specs=options.pop("out_specs", [space] * len(shapes)),
        compiler_params=pltpu.CompilerParams(vmem_limit_bytes=vmem),
        cost_estimate=pl.CostEstimate(flops=flops, bytes_accessed=moved, transcendentals=0),
        name=name,
        **options,
    )(*args)


def send_home(keep, send, extra, before):
    def array(*shape):
        return jax.ShapeDtypeStruct(shape, jnp.bfloat16)

    rows, columns = keep.shape[3:]
    pair, single = array(2, rows, columns), array(rows, columns)
    mark = jax.ShapeDtypeStruct((8, 128), jnp.float32)
    got = swap(send, "dp", 1)
    away_out, away_grad, home, mark_cores = call_kernel(
        add_cores, "add_cores", [pair, pair, array(2, 2, rows, columns), mark], [keep, got]
    )
    away = (swap(away_out, "dp", 2), swap(away_grad, "expert", 1))
    *lasts, mark_first = call_kernel(add_first, "add_first", [single, single, mark], [home, *away, *before])
    last = (swap(lasts[0], "expert", 1), swap(lasts[1], "dp", 2))
    total, mark_last = call_kernel(
        functools.partial(add_last, len(extra)),
        "add_last",
        [pair, mark],
        [home, *away, *last, *extra],
    )
    return total, mark_last


def take_rows(kind, pick_ref, pieces, store):
    for x in range(2):
        for core in range(2):
            half, rest, across, *last = pieces[core * len(pieces) // 2 : (core + 1) * len(pieces) // 2]
            if x == 0:
                block = jnp.concatenate([half[kind], rest[kind]], axis=0)
            else:
                rows = last[kind][...] if len(last) == 2 else last[0][kind]
                block = jnp.concatenate([across[kind], rows], axis=0)
            store(2 * x + core, mxu(pick_ref[x, core], block))


def spread_rows(kind, part, half, rows, place_ref, keep_ref, send_ref):
    capacity = rows.shape[0] // 4
    side = half ^ part
    for x in range(2):
        for core in range(2):
            group = 2 * x + core
            piece = rows[group * capacity : (group + 1) * capacity]
            out = mxu(place_ref[x, core], piece).astype(jnp.bfloat16)
            target = keep_ref if core == 0 else send_ref
            if kind == 0:
                target[kind, x, side] = out
            else:
                target[kind, side, x] = out


def chunk_kernel(step, count, part_ref, pick_ref, place_ref, scale_ref, *refs):
    sources, refs = refs[:count], refs[-17 - count :]
    outs, saved = refs[:2], refs[2:7]
    kept, buffers = refs[7:12], refs[12 : 12 + count]
    homes, sems = refs[-5:-3], refs[-3:]
    keep_ref, send_ref = homes
    rows_ref, cot_ref, hidden_ref, d_gate_ref, d_up_ref = kept
    pieces, (w_gate, w_up, w_down) = buffers[:-3], buffers[-3:]
    rows, capacity = rows_ref.shape[0], pick_ref.shape[2]
    def piece_loads(kind):
        copies = []
        for i, (source, target) in enumerate(zip(sources[:-3], pieces)):
            if len(source.shape) == 3:
                source, target = source.at[kind], target.at[kind]
            elif i % 5 != 3 + kind:
                continue
            copies.append(pltpu.make_async_copy(source, target, sems[0].at[kind, i]))
        return copies

    weight_loads = [
        pltpu.make_async_copy(source, target, sems[0].at[0, count - 3 + i])
        for i, (source, target) in enumerate(zip(sources[-3:], buffers[-3:]))
    ]
    stores = [
        pltpu.make_async_copy(source, target.at[pl.ds(step * rows, rows)], sems[1].at[i])
        for i, (source, target) in enumerate(zip(kept, saved))
    ]
    sends = [
        pltpu.make_async_copy(source.at[kind], target.at[kind], sems[2].at[kind, i])
        for kind in range(2)
        for i, (source, target) in enumerate(zip(homes, outs))
    ]
    token_loads, cot_loads = piece_loads(0), piece_loads(1)
    for copy in [*token_loads, *weight_loads[:2], weight_loads[2], *cot_loads]:
        copy.start()

    def store_rows(group, found):
        rows_ref[pl.ds(group * capacity, capacity), :] = found.astype(jnp.bfloat16)

    def store_cot(group, found):
        span = pl.ds(group * capacity, capacity)
        cot_ref[span, :] = (found * scale_ref[span, :]).astype(jnp.bfloat16)

    part = part_ref[0]
    width = w_down.shape[1] // 2
    halves = [slice(half * width, (half + 1) * width) for half in range(2)]
    for copy in token_loads:
        copy.wait()
    take_rows(0, pick_ref, pieces, store_rows)
    stores[0].start()
    expert_in = rows_ref[...]
    weight_loads[0].wait()
    gate_val = mxu(expert_in, w_gate[...])
    weight_loads[1].wait()
    up_val = mxu(expert_in, w_up[...])
    act_val, act_slope = silu_parts(gate_val)
    hidden = (act_val * up_val).astype(jnp.bfloat16)
    hidden_ref[...] = hidden
    stores[2].start()
    weight_loads[2].wait()
    for half, span in enumerate(halves):
        out = (mxu(hidden, w_down[:, span]) * scale_ref[...]).astype(jnp.bfloat16)
        spread_rows(0, part, half, out, place_ref, keep_ref, send_ref)
    for send in sends[:2]:
        send.start()
    for copy in cot_loads:
        copy.wait()
    take_rows(1, pick_ref, pieces, store_cot)
    stores[1].start()
    d_hidden = mxu(cot_ref[...], w_down[...], ((1,), (1,)))
    d_gate = (d_hidden * up_val * act_slope).astype(jnp.bfloat16)
    d_up = (d_hidden * act_val).astype(jnp.bfloat16)
    d_gate_ref[...] = d_gate
    d_up_ref[...] = d_up
    stores[3].start()
    stores[4].start()
    for half, span in enumerate(halves):
        grad = mxu(d_gate, w_gate[span, :], ((1,), (1,))) + mxu(d_up, w_up[span, :], ((1,), (1,)))
        spread_rows(1, part, half, grad.astype(jnp.bfloat16), place_ref, keep_ref, send_ref)
    for send in sends[2:]:
        send.start()
    for copy in stores + sends:
        copy.wait()


def run_chunk(step, tables, sources, saved_shapes, saved, marks):
    def array(a):
        return jax.ShapeDtypeStruct(a.shape, a.dtype)

    def scratch(a):
        return pltpu.VMEM(a.shape, a.dtype)

    kinds, half_rows, model_width = sources[0].shape
    home = jax.ShapeDtypeStruct((kinds, 2, 2, 2 * half_rows, model_width // 2), jnp.bfloat16)
    vmem, hbm = pl.BlockSpec(memory_space=pltpu.VMEM), pl.BlockSpec(memory_space=pl.ANY)
    rows = tables[-1].shape[0]
    first_saved = len(tables) + len(sources)
    return call_kernel(
        functools.partial(chunk_kernel, step, len(sources)),
        "chunk",
        [home, home, *saved_shapes],
        [*tables, *sources, *saved, *marks],
        vmem=60 * 2**20,
        flops=12 * rows * sources[-1].shape[0] * sources[-1].shape[1],
        in_specs=[pl.BlockSpec(memory_space=pltpu.SMEM)]
        + [vmem] * (len(tables) - 1)
        + [hbm] * (len(sources) + len(saved))
        + [vmem] * len(marks),
        out_specs=[hbm] * (2 + len(saved_shapes)),
        input_output_aliases={first_saved + i: 2 + i for i in range(len(saved))},
        scratch_shapes=[pltpu.VMEM((rows, s.shape[1]), s.dtype) for s in saved_shapes]
        + [scratch(source) for source in sources]
        + [scratch(home)] * 2
        + [pltpu.SemaphoreType.DMA(n) for n in ((2, len(sources)), (len(saved_shapes),), (2, 2))],
    )


def dense_plan(tokens, routes, kept_mask, gate_probs, output_grad, w_gate, w_up, w_down):
    dp_size = lax.axis_size("dp")
    line = dp_size // 4
    tok_rows, top_count = routes.shape
    capacity = tok_rows * top_count // dp_size
    model_width = tokens.shape[1]
    hidden_part = w_gate.shape[2]
    rows = 4 * capacity
    part = lax.axis_index("expert")
    w_gate, w_up, w_down = w_gate[0], w_up[0], w_down[0]

    table = jnp.concatenate(
        [routes.T.astype(jnp.float32), kept_mask.T.astype(jnp.float32), gate_probs.T], axis=0
    )
    part_arg = part.astype(jnp.int32).reshape(1)
    mine, other, table = own_halves(part_arg, tokens, output_grad, table)
    table = gather_small(table, line)
    chosen, kept, probs = jnp.split(table, 3, axis=3)
    expert = lax.axis_index("dp").astype(jnp.float32)
    hit = jnp.where(chosen == expert, kept, 0.0)
    used = jnp.sum(hit, axis=3)
    weight = jnp.sum(hit * probs, axis=3)
    kept_count = jnp.sum(used)
    earlier = jnp.triu(jnp.ones((tok_rows, tok_rows), jnp.bfloat16), 1)
    rank = jnp.einsum(
        "sabt,tu->sabu", used.astype(jnp.bfloat16), earlier, preferred_element_type=jnp.float32
    )
    slots = jnp.arange(capacity, dtype=jnp.float32)[:, None]
    pick = jnp.where(rank[..., None, :] == slots, used[..., None, :], 0.0)
    row_weight = jnp.sum(pick * weight[..., None, :], axis=4).reshape(line, rows, 1)
    pick = pick.astype(jnp.bfloat16)
    place = jnp.swapaxes(pick, 3, 4)
    pick_in = jnp.where(part == 0, pick, jnp.roll(pick, tok_rows // 2, axis=4))


    def saved_array(width):
        return jax.ShapeDtypeStruct((line * rows, width), jnp.bfloat16)

    saved_shapes = [saved_array(model_width)] * 2 + [saved_array(hidden_part)] * 3
    done = []

    def chunk(step, rows_in):
        saved = done[-1][2:] if done else []
        done.append(
            run_chunk(
                step,
                [part_arg, pick_in[step], place[step], row_weight[step]],
                [*rows_in, w_gate, w_up, w_down],
                saved_shapes,
                saved,
                [],
            )
        )
        return done[-1][1]

    pieces = gather_line(mine, other, line, functools.partial(chunk, 0))
    for step in range(1, line):
        chunk(step, pieces[step])
    saved = done[-1][2:]

    down, up, before = [], [], []
    for step in range(line // 2, 0, -1):
        total, mark = send_home(*done[step][:2], down, [])
        before = before or [mark]
        down = [shift(total, -1)]
    for step in range(line // 2 + 1, line):
        up = [shift(send_home(*done[step][:2], up, before)[0], 1)]
    returns = [send_home(*done[0][:2], [], [])[0], *down, *up]
    expert_in, cot_rows, hidden, d_gate, d_up = saved
    inv_count = 1.0 / jnp.maximum(kept_count, 1.0)
    by_row = ((0,), (0,))
    grad_down = (mxu(hidden, cot_rows, by_row) * inv_count).astype(jnp.bfloat16)
    grad_gate = (mxu(expert_in, d_gate, by_row) * inv_count).astype(jnp.bfloat16)
    grad_up = (mxu(expert_in, d_up, by_row) * inv_count).astype(jnp.bfloat16)
    results = sum(total.astype(jnp.float32) for total in returns).astype(jnp.bfloat16)
    return (results[0], results[1], grad_gate[None], grad_up[None], grad_down[None])


def per_device(tokens, routes, kept_mask, gate_probs, output_grad, w_gate, w_up, w_down):
    dp_size = lax.axis_size("dp")
    local_experts = w_gate.shape[0]
    top_count = routes.shape[1]
    dense = (
        local_experts == 1
        and lax.axis_size("expert") == 2
        and dp_size % 4 == 0
        and 2 * top_count >= dp_size
    )
    plan = dense_plan if dense else routed_plan
    return plan(tokens, routes, kept_mask, gate_probs, output_grad, w_gate, w_up, w_down)


def solution(mesh):
    placed = (
        P("dp", None),
        P("dp", None),
        P("dp", None),
        P("dp", None),
        P("dp", None),
        P("dp", None, "expert"),
        P("dp", None, "expert"),
        P("dp", "expert", None),
    )
    return jax.shard_map(
        per_device,
        mesh=mesh,
        in_specs=placed,
        out_specs=(
            P("dp", "expert"),
            P("dp", "expert"),
            P("dp", None, "expert"),
            P("dp", None, "expert"),
            P("dp", "expert", None),
        ),
        check_vma=False,
    )
```
